256 devices in a mesh: seq: 32 (over z, x), exp: 8 (over y, core).
Axes of the slice: x: 4, y: 4, z: 8, core: 2. Of those that a mesh axis runs over, the one named last changes fastest.
Arguments:
- residual: bfloat16 [4096, 4096], P('seq', 'exp'), may hold values from -6 to 6
- query_proj: bfloat16 [4096, 4096], P('seq', 'exp'), may hold values from -6 to 6
- key_proj: bfloat16 [4096, 4096], P('seq', 'exp'), may hold values from -6 to 6
- value_proj: bfloat16 [4096, 4096], P('seq', 'exp'), may hold values from -6 to 6
- short_kernel: float32 [3, 3, 4096], P(None, None, 'exp'), may hold values from -3 to 3
- filter_raw: float32 [4096, 8, 512], P(None, 'exp', 'seq'), may hold values from -6 to 6
- filter_decay: float32 [8, 512], P('exp', 'seq'), may hold values from 4.8828124e-06 to 0.03
- routes: int32 [4096, 2], P('seq'), may hold values from 0 to 7, all different within a row; in each aligned block of 128 rows (0 to 127, 128 to 255, ...) at most 40 rows name the same one
- gate_weights: float32 [4096, 2], P('seq'), may hold values from 0.3 to 1
- norm_gain: float32 [4096], replicated, may hold values from 0.5 to 1.5
- w_gate: bfloat16 [8, 4096, 11008], P('exp', None, 'seq'), may hold values from -0.09375 to 0.09375
- w_up: bfloat16 [8, 4096, 11008], P('exp', None, 'seq'), may hold values from -0.09375 to 0.09375
- w_down: bfloat16 [8, 11008, 4096], P('exp', 'seq'), may hold values from -0.0546875 to 0.0546875
Outputs:
- block_out: bfloat16 [4096, 4096], P('seq', 'exp')
The draws below stay inside these ranges and needn't reach their ends.
Inputs may be any that keep to these rules, and one draw needn't show every extreme that they name: `routes`: the 2 ids of a row differ. In each aligned block of 128 rows (the tokens of one index of seq) no expert is named by more than 40 rows, a bound that some block reaches.
All inputs are finite; a program needn't handle non-finite values.
Results may differ from the reference program's by a relative error of at most 0.015.
Values may be sent and summed in bfloat16 or wider, within the bound.
A program may use at most 128 MiB of HBM per device.

```python
import math
import jax
import jax.numpy as jnp
import numpy as np
from jax import lax

D = 4096
FF = 11008
TOPK = 2
SHORT = 3
TOK_DEV = 128
TOKENS = 4096
EXPERTS = 8
CAP = 40
N_SEQ = 32
N_EXP = 8


def levels(own_key, shape, shards, least, top_value):
    gain = 1.0
    for position, blocks in shards:
        draws = jax.random.uniform(jax.random.fold_in(jax.random.fold_in(own_key, 6), position), (blocks,), jnp.float32, least / len(shards), top_value / len(shards))
        gain = gain * jnp.repeat(jnp.exp(draws), shape[position] // blocks).reshape((-1,) + (1,) * (len(shape) - 1 - position))
    return gain


def deal_out(own_key, own, number, rows, amount, top, most, skew):
    ranking = jax.random.permutation(own_key, amount)
    heavy_load, common = shares(amount, rows * top, most, skew, True), shares(amount, rows * top, most, skew, False)
    places = jnp.arange(amount)

    def named(lengths, turn):
        used = int((lengths > 0).sum())
        fixed = max(1, used // 4)
        shifted = fixed + (places - fixed + turn * (used - fixed)) % max(1, amount - fixed)
        return jnp.zeros((amount,), jnp.int32).at[ranking[jnp.where(places < fixed, places, shifted)]].set(jnp.asarray(lengths, jnp.int32))

    lengths = jnp.where(number % 4 == 0, named(heavy_load, number // 4), named(common, number - number // 4 - 1))
    mixed = jax.random.permutation(jax.random.fold_in(own, 3), amount)
    source_of, receiver = mixed[0:amount // 2 * 2:2], mixed[1:amount // 2 * 2:2]
    slack = jnp.minimum(lengths[source_of] - 1, most - lengths[receiver]) // 2
    slack = jnp.where((source_of == ranking[0]) | (receiver == ranking[0]) | (lengths[receiver] == 0), 0, jnp.maximum(slack, 0))
    shifted = jax.random.randint(jax.random.fold_in(own, 4), (amount // 2,), 0, 1 << 20) % (slack + 1)
    lengths = lengths.at[source_of].add(-shifted).at[receiver].add(shifted)
    members = jnp.searchsorted(jnp.cumsum(lengths), jnp.arange(rows * top), side="right").astype(jnp.int32)
    grid = members.reshape(top, rows).T
    grid = grid[jax.random.permutation(jax.random.fold_in(own, 1), rows)]
    turn = jax.random.randint(jax.random.fold_in(own, 2), (rows, 1), 0, top)
    return jnp.take_along_axis(grid, (jnp.arange(top)[None, :] + turn) % top, axis=1)


def shares(count, total, most, skew, full):
    portions = [(1 << 20) // math.isqrt(rank ** skew) + 1 for rank in range(1, count + 1)]
    largest = most if full else min(most, max(-(-total // count), total * portions[0] // sum(portions)))
    least = 1 if total - largest >= count - 1 else 0
    holding, surplus = [largest] + [least] * (count - 1), total - largest - least * (count - 1)
    while surplus > 0:
        movable = [i for i in range(1, count) if holding[i] < largest] or [i for i in range(1, count) if holding[i] < most]
        pool, left = sum([portions[i] for i in movable]), surplus
        for i in movable:
            more = min(most - holding[i], max(1, left * portions[i] // pool), surplus)
            holding[i] = holding[i] + more
            surplus = surplus - more
    return np.array(holding)


def noise(key, dims, width, most, pieces=(), kind=jnp.bfloat16):
    drawn = width * jax.random.normal(key, dims, jnp.float32)
    if pieces:
        drawn = drawn * levels(key, dims, pieces, -0.22, 0.18)
    return jnp.clip(drawn, -most, most).astype(kind)


def setup_inputs(seed: int = 0) -> dict:
    seeds = jax.random.split(jax.random.key(seed), 14)
    residual = noise(seeds[0], (TOKENS, D), 1.0, 6.0, ((0, 32), (1, 8)))
    query_proj = noise(seeds[1], (TOKENS, D), 1.0, 6.0, ((0, 32), (1, 8)))
    key_proj = noise(seeds[2], (TOKENS, D), 1.0, 6.0, ((0, 32), (1, 8)))
    value_proj = noise(seeds[3], (TOKENS, D), 1.0, 6.0, ((0, 32), (1, 8)))
    short_kernel = noise(seeds[4], (3, SHORT, D), 0.6, 3.0, ((2, 8),), jnp.float32)
    filter_raw = noise(seeds[5], (TOKENS, N_EXP, D // N_EXP), 1.0, 6.0, ((1, 8), (2, 32)), jnp.float32)
    filter_decay = jnp.clip(jnp.exp(math.log(0.03) - 8.723231 * jax.random.uniform(seeds[6], (N_EXP, D // N_EXP), jnp.float32) ** levels(seeds[6], (N_EXP, D // N_EXP), ((0, 8), (1, 32)), -0.2, 0.2)), 4.882812390860636e-06, 0.03)
    routes_keys = jax.random.split(jax.random.fold_in(seeds[7], 1), TOKENS // TOK_DEV)
    routes_turns = jax.random.permutation(jax.random.fold_in(seeds[7], 3), TOKENS // TOK_DEV)
    routes = jax.vmap(lambda own, number: deal_out(jax.random.fold_in(seeds[7], 2), own, number, TOK_DEV, EXPERTS, TOPK, CAP, 2))(routes_keys, routes_turns).reshape((TOKENS, TOPK))
    gate_weights = jnp.clip(0.3 + 0.7 * jax.random.uniform(seeds[8], (TOKENS, TOPK), jnp.float32) ** levels(seeds[8], (TOKENS, TOPK), ((0, 32),), -0.2, 0.2), 0.3, 1.0)
    norm_gain = jnp.clip(jax.random.uniform(seeds[9], (D,), jnp.float32, 0.5, 1.5), 0.5, 1.5)
    w_gate = noise(seeds[10], (EXPERTS, D, FF), D ** -0.5, 0.09375, ((0, 8), (2, 32)))
    w_up = noise(seeds[11], (EXPERTS, D, FF), D ** -0.5, 0.09375, ((0, 8), (2, 32)))
    w_down = noise(seeds[12], (EXPERTS, FF, D), FF ** -0.5, 0.0546875, ((0, 8), (1, 32)))
    return {"residual": residual, "query_proj": query_proj, "key_proj": key_proj, "value_proj": value_proj, "short_kernel": short_kernel, "filter_raw": filter_raw, "filter_decay": filter_decay, "routes": routes, "gate_weights": gate_weights, "norm_gain": norm_gain, "w_gate": w_gate, "w_up": w_up, "w_down": w_down}


def short_filter(extended, kernel, length):
    tap_count = kernel.shape[0]
    signal = extended.astype(jnp.float32)
    running = kernel[0] * signal[tap_count - 1:tap_count - 1 + length]
    for offset in range(1, tap_count):
        running = running + kernel[offset] * signal[tap_count - 1 - offset:tap_count - 1 - offset + length]
    return running

def with_zeros(signal, tap_count):
    return jnp.concatenate((jnp.zeros((tap_count - 1, signal.shape[1]), signal.dtype), signal), axis=0)

def long_filter(raw_taps, decay_rate, length):
    positions = jnp.arange(length).astype(jnp.float32)[:, None]
    energy = jnp.expm1(-2.0 * decay_rate * length) / jnp.expm1(-2.0 * decay_rate)
    return raw_taps * jnp.exp(-decay_rate * positions) / jnp.sqrt(energy)

def rms_rows(rows_in, norm_gain):
    values = rows_in.astype(jnp.float32)
    square = lax.optimization_barrier(jnp.mean(values * values, axis=-1, keepdims=True))
    return (values * lax.rsqrt(square + 1e-06) * norm_gain).astype(jnp.bfloat16)

def reference(residual, query_proj, key_proj, value_proj, short_kernel, filter_raw, filter_decay, routes, gate_weights, norm_gain, w_gate, w_up, w_down):
    query_short = short_filter(with_zeros(query_proj, SHORT), short_kernel[0], TOKENS)
    key_short = short_filter(with_zeros(key_proj, SHORT), short_kernel[1], TOKENS)
    value_short = short_filter(with_zeros(value_proj, SHORT), short_kernel[2], TOKENS)
    zed = (key_short * value_short).astype(jnp.bfloat16)
    taps = long_filter(filter_raw.reshape(TOKENS, D), filter_decay.reshape(D), TOKENS)
    padded_size = 2 * TOKENS
    spectrum = jnp.fft.rfft(zed.astype(jnp.float32), padded_size, axis=0) * jnp.fft.rfft(taps, padded_size, axis=0)
    conv = jnp.fft.irfft(spectrum, padded_size, axis=0)[:TOKENS].astype(jnp.bfloat16)
    mixed = (residual.astype(jnp.float32) + query_short * conv.astype(jnp.float32)).astype(jnp.bfloat16)
    normed = rms_rows(mixed, norm_gain)
    expert_ids = jnp.arange(EXPERTS, dtype=jnp.int32)
    expert_hot = (routes[:, :, None] == expert_ids).astype(jnp.int32)
    per_token = lax.optimization_barrier(jnp.sum(expert_hot, axis=1)).reshape(N_SEQ, TOK_DEV, EXPERTS)
    earlier = (jnp.cumsum(per_token, axis=1) - per_token).reshape(TOKENS, EXPERTS)
    slot_index = lax.optimization_barrier(jnp.sum(expert_hot * earlier[:, None, :], axis=2)).astype(jnp.int32)
    block_index = jnp.arange(TOKENS, dtype=jnp.int32) // TOK_DEV
    buffer_row = (block_index[:, None] * CAP + slot_index).astype(jnp.int32)
    sent_rows = jnp.broadcast_to(normed[:, None, :], (TOKENS, TOPK, D)).reshape(TOKENS * TOPK, D)
    buffers = jnp.zeros((EXPERTS, N_SEQ * CAP, D), jnp.bfloat16).at[routes.reshape(-1), buffer_row.reshape(-1)].set(sent_rows)
    group_width = FF // N_SEQ

    def run_expert(operands):
        rows_in, gate_mat, up_mat, down_mat = operands
        gate_act = jnp.dot(rows_in, gate_mat, preferred_element_type=jnp.float32)
        up_act = jnp.dot(rows_in, up_mat, preferred_element_type=jnp.float32)
        hidden = (jax.nn.silu(gate_act) * up_act).astype(jnp.bfloat16)
        hidden_groups = hidden.reshape(N_SEQ * CAP, N_SEQ, group_width).transpose(1, 0, 2)
        down_groups = down_mat.reshape(N_SEQ, group_width, D)

        def add_group(running, pair):
            partial_sum = jnp.dot(pair[0], pair[1], preferred_element_type=jnp.float32).astype(jnp.bfloat16)
            partial_sum = lax.optimization_barrier(partial_sum)
            return (running + partial_sum.astype(jnp.float32), None)
        summed, _ = lax.scan(add_group, jnp.zeros((N_SEQ * CAP, D), jnp.float32), (hidden_groups, down_groups))
        return summed.astype(jnp.bfloat16)
    expert_results = lax.map(run_expert, (buffers, w_gate, w_up, w_down))
    picked = expert_results[routes, buffer_row]
    combined = lax.optimization_barrier(jnp.sum(gate_weights[:, :, None] * picked.astype(jnp.float32), axis=1))
    return (mixed.astype(jnp.float32) + combined).astype(jnp.bfloat16)
```

```python
import functools
import math

import jax
import jax.numpy as jnp
from jax import lax
from jax.experimental import pallas as pl
from jax.experimental.pallas import tpu as pltpu
from jax.sharding import PartitionSpec as P

MESH = pl.DeviceIdType.MESH
F32, BF16 = jnp.float32, jnp.bfloat16


def passed_along(value, axis, by):
    devices = lax.axis_size(axis)
    pairs = [(i, i + by) for i in range(devices) if 0 <= i + by < devices]
    return lax.ppermute(value, axis, pairs)


def short_filter(extended, kernel, length):
    tap_count = kernel.shape[0]
    signal = extended.astype(jnp.float32)
    running = kernel[0] * signal[tap_count - 1 : tap_count - 1 + length]
    for offset in range(1, tap_count):
        running = (
            running
            + kernel[offset] * signal[tap_count - 1 - offset : tap_count - 1 - offset + length]
        )
    return running


def with_zeros(signal, tap_count):
    return jnp.concatenate(
        (jnp.zeros((tap_count - 1, signal.shape[1]), signal.dtype), signal), axis=0
    )


def long_filter(raw_taps, decay_rate, length):
    positions = jnp.arange(length).astype(jnp.float32)[:, None]
    energy = jnp.expm1(-2.0 * decay_rate * length) / jnp.expm1(-2.0 * decay_rate)
    return raw_taps * jnp.exp(-decay_rate * positions) / jnp.sqrt(energy)


def angle_table(row_total, col_total, period):
    product = (
        jnp.arange(row_total, dtype=jnp.int32)[:, None]
        * jnp.arange(col_total, dtype=jnp.int32)[None, :]
        % period
    )
    theta = product.astype(jnp.float32) * (2.0 * math.pi / period)
    return (jnp.cos(theta), jnp.sin(theta))


def left_real(tables, direction, real_part):
    cosine, sine = tables
    highest = lax.Precision.HIGHEST
    cos_real = jnp.einsum("kn,cnm->ckm", cosine, real_part, precision=highest)
    sin_real = jnp.einsum("kn,cnm->ckm", sine, real_part, precision=highest)
    return (cos_real, -direction * sin_real)


def left_real_out(tables, direction, real_part, imag_part):
    cosine, sine = tables
    highest = lax.Precision.HIGHEST
    cos_real = jnp.einsum("kn,cnm->ckm", cosine, real_part, precision=highest)
    sin_imag = jnp.einsum("kn,cnm->ckm", sine, imag_part, precision=highest)
    return cos_real + direction * sin_imag


def right_apply(tables, direction, real_part, imag_part):
    cosine, sine = tables
    highest = lax.Precision.HIGHEST
    cos_real = jnp.einsum("ckn,nm->ckm", real_part, cosine, precision=highest)
    cos_imag = jnp.einsum("ckn,nm->ckm", imag_part, cosine, precision=highest)
    sin_real = jnp.einsum("ckn,nm->ckm", real_part, sine, precision=highest)
    sin_imag = jnp.einsum("ckn,nm->ckm", imag_part, sine, precision=highest)
    return (cos_real + direction * sin_imag, cos_imag - direction * sin_real)


def twist(tables, direction, real_part, imag_part):
    cosine, sine = tables
    return (
        real_part * cosine + direction * imag_part * sine,
        imag_part * cosine - direction * real_part * sine,
    )


def causal_conv(signal, taps):
    channel_count, length = signal.shape
    padded_size = 2 * length
    second = 128
    first = padded_size // second
    first_tab = angle_table(first, first, first)
    second_tab = angle_table(second, second, second)
    twist_tab = angle_table(first, second, padded_size)
    both = jnp.concatenate((signal, taps), axis=0)
    real_part = jnp.pad(both, ((0, 0), (0, length))).reshape(2 * channel_count, first, second)
    real_part, imag_part = left_real(first_tab, 1.0, real_part)
    real_part, imag_part = twist(twist_tab, 1.0, real_part, imag_part)
    real_part, imag_part = right_apply(second_tab, 1.0, real_part, imag_part)
    sig_real, tap_real = (real_part[:channel_count], real_part[channel_count:])
    sig_imag, tap_imag = (imag_part[:channel_count], imag_part[channel_count:])
    prod_real = sig_real * tap_real - sig_imag * tap_imag
    prod_imag = sig_real * tap_imag + sig_imag * tap_real
    real_part, imag_part = right_apply(second_tab, -1.0, prod_real, prod_imag)
    real_part, imag_part = twist(twist_tab, -1.0, real_part, imag_part)
    real_part = left_real_out(first_tab, -1.0, real_part, imag_part)
    return real_part.reshape(channel_count, padded_size)[:, :length] / padded_size


def expert_kernel(
    dims,
    mixed_ref, place_ref, wmap_ref, gain_ref, wg_hbm, wu_hbm, wd_hbm, out_ref,
    wg, wu, wd, outg, arr, xa, xb, acc_g, acc_u, hid, pc, pd, rc1, rc2, rd1, rd2, yb, ret,
    w_sem, go_send, go_recv, a_recv, b_recv, rc1_recv, rc2_recv, rd1_recv, rd2_recv, back_send, back_recv,
    az_send, ax_send, bz_send, bx_send, cz_send, cx_send, dz_send, dx_send,
):
    nz, nx, ne, cap, wa, wb = dims
    width = 2 * (wa + wb)
    chunk = width // ne
    s, e = lax.axis_index("seq"), lax.axis_index("exp")
    z, x = s // nx, s % nx

    def along_z(d):
        return (((z + (1, nz - 1)[d]) % nz) * nx + x, e)

    def along_x(d):
        return (z * nx + (x + (1, nx - 1)[d]) % nx, e)

    def expert(i):
        return (s, (e + i) % ne)

    def remote(src, dst, send, recv, to):
        return pltpu.make_async_remote_copy(
            src_ref=src, dst_ref=dst, send_sem=send, recv_sem=recv, device_id=to, device_id_type=MESH
        )

    def arrived(dst, recv):
        remote(dst, dst, recv, recv, along_z(0)).wait_recv()

    def sent(src, send):
        remote(src, src, send, send, along_z(0)).wait_send()

    weights = [
        pltpu.make_async_copy(h.at[0], v, w_sem.at[i]) for i, (h, v) in enumerate(((wg_hbm, wg), (wu_hbm, wu), (wd_hbm, wd)))
    ]
    for copy in weights:
        copy.start()

    barrier = pltpu.get_barrier_semaphore()
    partners = [along_z(0), along_z(1), along_x(0), along_x(1)] + [expert(i) for i in range(1, ne)]
    for to in partners:
        pl.semaphore_signal(barrier, inc=1, device_id=to, device_id_type=MESH)
    picked = jnp.dot(place_ref[...], mixed_ref[...], preferred_element_type=F32)
    outg[...] = picked.reshape(ne, cap, chunk).astype(BF16)
    arr[e] = outg[e]
    acc_g[...] = jnp.zeros_like(acc_g)
    acc_u[...] = jnp.zeros_like(acc_u)
    pl.semaphore_wait(barrier, len(partners))

    for i in range(1, ne):
        remote(outg.at[(e + i) % ne], arr.at[e], go_send.at[i], go_recv.at[i], expert(i)).start()
    for i in range(1, ne):
        arrived(arr.at[(e + ne - i) % ne], go_recv.at[i])
    square = jnp.zeros((cap, 1), F32)
    for c in range(ne):
        values = arr[c].astype(F32)
        square += jnp.sum(values * values, axis=-1, keepdims=True)
    scale = lax.rsqrt(square / width + 1e-06)
    spans = []
    for d in range(2):
        spans.append((xa, pc, d, d * wa, wa))
        spans.append((xb, pd, d, 2 * wa + d * wb, wb))
    for c in range(ne):
        values = (arr[c].astype(F32) * scale * gain_ref[:, c * chunk : (c + 1) * chunk]).astype(BF16)
        for ref, _, d, start, size in spans:
            lo, hi = max(start, c * chunk), min(start + size, (c + 1) * chunk)
            if lo < hi:
                ref[d, 0, 0, :, lo - start : hi - start] = values[:, lo - c * chunk : hi - c * chunk]

    def a_along_z(d, t, j):
        remote(xa.at[d, t, j], xa.at[d, t + 1, j], az_send.at[d], a_recv.at[d, t + 1, j], along_z(d)).start()

    def a_along_x(d, j):
        remote(xa.at[d, 0, j], xa.at[d, 0, j + 1], ax_send.at[d], a_recv.at[d, 0, j + 1], along_x(d)).start()

    def b_along_z(d, t):
        remote(xb.at[d, t, 0], xb.at[d, t + 1, 0], bz_send.at[d], b_recv.at[d, t + 1, 0], along_z(d)).start()

    def b_along_x(d, t, j):
        remote(xb.at[d, t, j], xb.at[d, t, j + 1], bx_send.at[d], b_recv.at[d, t, j + 1], along_x(d)).start()

    for d in range(2):
        b_along_z(d, 0)
        a_along_x(d, 0)
    for d in range(2):
        b_along_x(d, 0, 0)
        a_along_z(d, 0, 0)

    def turned(j, d):
        return (nx - j) % nx if d else j

    def rows_of(ref, d, t):
        parts = [ref[d, t, turned(j, d)].astype(F32) for j in range(nx)]
        return jnp.concatenate(parts, axis=0).astype(BF16)

    def group(d, t):
        return (nz - t) % nz if d else t

    def project(d, t):
        at = group(d, t)
        left, right = rows_of(xa, d, t), rows_of(xb, d, t)
        one = slice(d * wa, (d + 1) * wa)
        two = slice(2 * wa + d * wb, 2 * wa + (d + 1) * wb)
        for total, w in ((acc_g, wg), (acc_u, wu)):
            total[at] += jnp.dot(left, w[one, :], preferred_element_type=F32) + jnp.dot(
                right, w[two, :], preferred_element_type=F32
            )

    def activate(d, t):
        at = group(d, t)
        gate = acc_g[at]
        hid[at] = (gate / (1.0 + jnp.exp(-gate)) * acc_u[at]).astype(BF16)

    def gather_step(p, carry):
        for d in range(2):
            @pl.when(p <= nz - 1)
            def _():
                arrived(xb.at[d, p, 0], b_recv.at[d, p, 0])
                b_along_x(d, p, 0)

            @pl.when(p < nz - 1)
            def _():
                b_along_z(d, p)

            @pl.when(p <= nx - 1)
            def _():
                arrived(xa.at[d, 0, p], a_recv.at[d, 0, p])
                a_along_z(d, 0, p)

            @pl.when(p < nx - 1)
            def _():
                a_along_x(d, p)

        for j in range(nx):
            for d in range(2):
                t = p - j

                @pl.when((t >= 1) & (t <= nz - 1))
                def _():
                    arrived(xa.at[d, t, j], a_recv.at[d, t, j])

                @pl.when((t >= 1) & (t < nz - 1))
                def _():
                    a_along_z(d, t, j)

            if j >= 1:
                for d in range(2):
                    t = p - j

                    @pl.when((t >= 0) & (t <= nz - 1))
                    def _():
                        arrived(xb.at[d, t, j], b_recv.at[d, t, j])
                        if j < nx - 1:
                            b_along_x(d, t, j)

        @pl.when(p == nx - 1)
        def _():
            for copy in weights:
                copy.wait()

        for d in range(2):
            t = p - (nx - 1)

            @pl.when(t >= 0)
            def _():
                project(d, t)

            @pl.when((t > nz // 2) | ((t == 0) | (t == nz // 2)) & (d == 1))
            def _():
                activate(d, t)

        return carry

    lax.fori_loop(1, nz + nx - 1, gather_step, 0)

    def down(d, q):
        at = group(d, q % nz)
        rows = hid[at]
        for ref, start, size in ((pc, d * wa, wa), (pd, 2 * wa + d * wb, wb)):
            part = jnp.dot(rows, wd[:, start : start + size], preferred_element_type=F32)
            for j in range(nx):
                ref[d, q - 1, turned(j, d)] = part[j * cap : (j + 1) * cap].astype(BF16)

    def add(total, more):
        total[...] = (total[...].astype(F32) + more[...].astype(F32)).astype(BF16)

    for d in range(2):
        down(d, 1)

    def reduce_step(p, carry):
        for d in range(2):
            for v in range(1, nx + 1):
                k, j = p - v + 1, v % nx

                @pl.when((k >= 1) & (k <= nz))
                def _():
                    if v >= 2:
                        arrived(rd1.at[d, v - 2, k - 1], rd1_recv.at[d, v - 2, k - 1])
                        add(pd.at[d, k - 1, j], rd1.at[d, v - 2, k - 1])
                    if v < nx:
                        remote(
                            pd.at[d, k - 1, j], rd1.at[d, v - 1, k - 1], dx_send.at[d], rd1_recv.at[d, v - 1, k - 1], along_x(d)
                        ).start()
                    else:
                        @pl.when(k >= 2)
                        def _():
                            arrived(rd2.at[d, k - 2], rd2_recv.at[d, k - 2])
                            add(pd.at[d, k - 1, 0], rd2.at[d, k - 2])

                        @pl.when(k < nz)
                        def _():
                            remote(
                                pd.at[d, k - 1, 0], rd2.at[d, k - 1], dz_send.at[d], rd2_recv.at[d, k - 1], along_z(d)
                            ).start()

        for d in range(2):
            for v in range(1, nx + 1):
                q, j = p - v + 1, v % nx

                @pl.when((q >= 2) & (q <= nz))
                def _():
                    arrived(rc1.at[d, q - 2, j], rc1_recv.at[d, q - 2, j])
                    add(pc.at[d, q - 1, j], rc1.at[d, q - 2, j])

                @pl.when((q >= 1) & (q < nz))
                def _():
                    remote(
                        pc.at[d, q - 1, j], rc1.at[d, q - 1, j], cz_send.at[d], rc1_recv.at[d, q - 1, j], along_z(d)
                    ).start()

                @pl.when(q == nz)
                def _():
                    if v >= 2:
                        arrived(rc2.at[d, v - 2], rc2_recv.at[d, v - 2])
                        add(pc.at[d, nz - 1, j], rc2.at[d, v - 2])
                    if v < nx:
                        remote(
                            pc.at[d, nz - 1, j], rc2.at[d, v - 1], cx_send.at[d], rc2_recv.at[d, v - 1], along_x(d)
                        ).start()

        for d in range(2):
            @pl.when(p < nz)
            def _():
                down(d, p + 1)

        return carry

    lax.fori_loop(1, nz + nx, reduce_step, 0)

    for c in range(ne):
        for _, ref, d, start, size in spans:
            lo, hi = max(start, c * chunk), min(start + size, (c + 1) * chunk)
            if lo < hi:
                yb[c, :, lo - c * chunk : hi - c * chunk] = ref[d, nz - 1, 0, :, lo - start : hi - start]
    for i in range(1, ne):
        remote(yb.at[(e + i) % ne], ret.at[e], back_send.at[i], back_recv.at[i], expert(i)).start()
    ret[e] = yb[e]
    for d in range(2):
        sent(xa.at[d, 0 : nz - 1], az_send.at[d])
        sent(xa.at[d, 0, 0 : nx - 1], ax_send.at[d])
        sent(xb.at[d, 0 : nz - 1, 0], bz_send.at[d])
        sent(xb.at[d, :, 0 : nx - 1], bx_send.at[d])
        sent(pc.at[d, 0 : nz - 1], cz_send.at[d])
        sent(pc.at[d, nz - 1, 0 : nx - 1], cx_send.at[d])
        sent(pd.at[d, 0 : nz - 1, 0], dz_send.at[d])
        sent(pd.at[d, :, 0 : nx - 1], dx_send.at[d])
    for i in range(1, ne):
        sent(outg.at[i], go_send.at[i])
    for i in range(1, ne):
        arrived(ret.at[(e + ne - i) % ne], back_recv.at[i])
    rows = ret[...].astype(F32).reshape(ne * cap, chunk)
    combined = jnp.dot(wmap_ref[...], rows, preferred_element_type=F32, precision=lax.Precision.HIGHEST)
    out_ref[...] = (mixed_ref[...].astype(F32) + combined).astype(BF16)
    for i in range(1, ne):
        sent(yb.at[i], back_send.at[i])


def experts(mixed, place, wmap, gain, w_gate, w_up, w_down, nz, nx, parts):
    ne = lax.axis_size("exp")
    cap = place.shape[0] // ne
    chunk = mixed.shape[1]
    width = ne * chunk
    wa, wb = parts
    hidden = w_gate.shape[2]
    vmem, dma = pltpu.VMEM, pltpu.SemaphoreType.DMA
    scratch = [
        vmem((width, hidden), BF16),
        vmem((width, hidden), BF16),
        vmem((hidden, width), BF16),
        vmem((ne, cap, chunk), BF16),
        vmem((ne, cap, chunk), BF16),
        vmem((2, nz, nx, cap, wa), BF16),
        vmem((2, nz, nx, cap, wb), BF16),
        vmem((nz, nx * cap, hidden), F32),
        vmem((nz, nx * cap, hidden), F32),
        vmem((nz, nx * cap, hidden), BF16),
        vmem((2, nz, nx, cap, wa), BF16),
        vmem((2, nz, nx, cap, wb), BF16),
        vmem((2, nz - 1, nx, cap, wa), BF16),
        vmem((2, nx - 1, cap, wa), BF16),
        vmem((2, nx - 1, nz, cap, wb), BF16),
        vmem((2, nz - 1, cap, wb), BF16),
        vmem((ne, cap, chunk), BF16),
        vmem((ne, cap, chunk), BF16),
        dma((3,)),
        dma((ne,)),
        dma((ne,)),
        dma((2, nz, nx)),
        dma((2, nz, nx)),
        dma((2, nz - 1, nx)),
        dma((2, nx - 1)),
        dma((2, nx - 1, nz)),
        dma((2, nz - 1)),
        dma((ne,)),
        dma((ne,)),
    ] + [dma((2,))] * 8
    return pl.pallas_call(
        functools.partial(expert_kernel, (nz, nx, ne, cap, wa, wb)),
        out_shape=jax.ShapeDtypeStruct(mixed.shape, BF16),
        in_specs=[pl.BlockSpec(memory_space=pltpu.VMEM)] * 4 + [pl.BlockSpec(memory_space=pl.ANY)] * 3,
        out_specs=pl.BlockSpec(memory_space=pltpu.VMEM),
        scratch_shapes=scratch,
        compiler_params=pltpu.CompilerParams(
            collective_id=1, has_side_effects=True, vmem_limit_bytes=60 * 1024 * 1024
        ),
    )(mixed, place, wmap, gain, w_gate, w_up, w_down)


def slot_keys(routes, expert_count, capacity):
    tokens = routes.shape[0]
    hot = (routes[:, :, None] == jnp.arange(expert_count, dtype=jnp.int32)).astype(F32)
    before = (jnp.arange(tokens)[:, None] > jnp.arange(tokens)[None, :]).astype(F32)
    earlier = jnp.dot(before, jnp.sum(hot, axis=1))
    slot = jnp.sum(hot * earlier[:, None, :], axis=2).astype(jnp.int32)
    return routes * capacity + slot


def slot_maps(routes, gate_weights, expert_count, capacity):
    keys = slot_keys(routes, expert_count, capacity)
    rows = jnp.arange(expert_count * capacity, dtype=jnp.int32)
    place = ((keys[None, :, 0] == rows[:, None]) | (keys[None, :, 1] == rows[:, None])).astype(BF16)
    wmap = sum(jnp.where(keys[:, k, None] == rows[None, :], gate_weights[:, k, None], 0.0) for k in range(2))
    return place, wmap


def on_device(
    residual,
    query_proj,
    key_proj,
    value_proj,
    short_kernel,
    filter_raw,
    filter_decay,
    routes,
    gate_weights,
    norm_gain,
    w_gate,
    w_up,
    w_down,
):
    row_count, width_here = query_proj.shape
    tap_count = short_kernel.shape[1]
    seq_total = lax.axis_size("seq")
    exp_total = lax.axis_size("exp")
    length = row_count * seq_total
    slice_width = width_here // seq_total
    stacked = query_proj[None]
    rims = passed_along(stacked[:, row_count - (tap_count - 1) :], "seq", 1)
    extended = jnp.concatenate((rims, stacked), axis=1)
    query_short = short_filter(extended[0], short_kernel[0], row_count)
    key_full, value_full = (
        lax.all_to_all(key_proj, "seq", split_axis=1, concat_axis=0, tiled=True),
        lax.all_to_all(value_proj, "seq", split_axis=1, concat_axis=0, tiled=True),
    )
    kernel_here = lax.dynamic_slice_in_dim(
        short_kernel, lax.axis_index("seq") * slice_width, slice_width, 2
    )
    key_short = short_filter(with_zeros(key_full, tap_count), kernel_here[1], length)
    value_short = short_filter(with_zeros(value_full, tap_count), kernel_here[2], length)
    zed = (key_short * value_short).astype(jnp.bfloat16)
    taps = long_filter(
        filter_raw.reshape(length, slice_width), filter_decay.reshape(slice_width), length
    )
    conv_cols = causal_conv(zed.astype(jnp.float32).T, taps.T)
    conv_here = conv_cols.T.astype(jnp.bfloat16)
    conv = lax.all_to_all(conv_here, "seq", split_axis=0, concat_axis=1, tiled=True)
    mixed = (residual.astype(jnp.float32) + query_short * conv.astype(jnp.float32)).astype(
        jnp.bfloat16
    )
    topk_count = routes.shape[1]
    capacity = 5 * row_count * topk_count // (4 * exp_total)
    place, wmap = slot_maps(routes, gate_weights, exp_total, capacity)
    return experts(mixed, place, wmap, norm_gain[None, :], w_gate, w_up, w_down, seq_total // 4, 4, (768, 1280))


def solution(mesh):
    in_specs = (
        P("seq", "exp"),
        P("seq", "exp"),
        P("seq", "exp"),
        P("seq", "exp"),
        P(None, None, "exp"),
        P(None, "exp", "seq"),
        P("exp", "seq"),
        P("seq", None),
        P("seq", None),
        P(),
        P("exp", None, "seq"),
        P("exp", None, "seq"),
        P("exp", "seq", None),
    )
    out_specs = P("seq", "exp")
    return jax.shard_map(
        on_device, mesh=mesh, in_specs=in_specs, out_specs=out_specs, check_vma=False
    )
```

```python
import functools

import jax
import jax.numpy as jnp
from jax import lax
from jax.experimental import pallas as pl
from jax.experimental.pallas import tpu as pltpu
from jax.sharding import PartitionSpec as P

MESH = pl.DeviceIdType.MESH
F32, BF16 = jnp.float32, jnp.bfloat16


def mixer_kernel(
    dims,
    res_ref, q_ref, k_ref, v_ref, filt_ref, raw_ref, decay_ref, root_ref, out_ref,
    ext, rims, edge, taps, toep, zsend, zrecv, zrows, zpad, crows, csend, crecv,
    rim_send, rim_recv, z_send, z_recv, c_send, c_recv,
):
    ns, tok, chans, tap_count = dims
    length = ns * tok
    s, e = lax.axis_index("seq"), lax.axis_index("exp")
    rim = rims.shape[1]

    def peer(i):
        return (s + i) % ns

    def remote(src, dst, send, recv, to):
        return pltpu.make_async_remote_copy(
            src_ref=src, dst_ref=dst, send_sem=send, recv_sem=recv, device_id=(to, e), device_id_type=MESH
        )

    barrier = pltpu.get_barrier_semaphore()

    def greet(i, carry):
        pl.semaphore_signal(barrier, inc=1, device_id=(peer(i), e), device_id_type=MESH)
        return carry

    lax.fori_loop(1, ns, greet, 0)

    for j, ref in enumerate((q_ref, k_ref, v_ref)):
        edge[j] = ref[tok - rim :, :]
        ext[j, 8 : 8 + tok] = ref[...].astype(F32)
    zpad[...] = jnp.zeros_like(zpad)
    position = lax.broadcasted_iota(jnp.int32, (chans, length), 1).astype(F32)
    scaled = raw_ref[...] * jnp.exp(-decay_ref[...] * position) / root_ref[...]
    for c in range(chans):
        taps[c] = jnp.broadcast_to(scaled[c : c + 1, :], (8, length))

    band = lax.broadcasted_iota(jnp.int32, (tok, tok), 1) >= lax.broadcasted_iota(jnp.int32, (tok, tok), 0)

    def bands(c, carry):
        before = jnp.zeros((tok, tok), F32)
        for k in range(ns):
            row = jnp.concatenate([taps[c, :, k * tok : (k + 1) * tok]] * (tok // 8), axis=0)
            turned = pltpu.roll(row, 0, axis=1, stride=1, stride_axis=0)
            full = jnp.where(band, turned, before)
            high = full.astype(BF16)
            toep[c, k * tok : (k + 1) * tok, :tok] = high
            toep[c, k * tok : (k + 1) * tok, tok:] = (full - high.astype(F32)).astype(BF16)
            before = turned
        return carry

    early = chans // 4
    lax.fori_loop(0, early, bands, 0)
    pl.semaphore_wait(barrier, ns - 1)

    rim_copy = remote(edge, rims, rim_send, rim_recv, peer(1))
    rim_copy.start()
    lax.fori_loop(early, 2 * early, bands, 0)
    rim_copy.wait()

    def short(j):
        return (
            filt_ref[j, 0:1, :] * ext[j, 8 : 8 + tok]
            + filt_ref[j, 1:2, :] * ext[j, 7 : 7 + tok]
            + filt_ref[j, 2:3, :] * ext[j, 6 : 6 + tok]
        )

    for j in range(3):
        ext[j, 0:8] = jnp.where(s == 0, 0.0, rims[j].astype(F32)[rim - 8 :])
    zed = (short(1) * short(2)).astype(BF16).astype(F32)
    zsend[...] = zed.T.astype(BF16).reshape(ns, chans, tok)
    zrecv[s] = zsend[s]

    def send_zed(i, carry):
        remote(zsend.at[peer(i)], zrecv.at[s], z_send, z_recv, peer(i)).start()
        return carry

    lax.fori_loop(1, ns, send_zed, 0)
    lax.fori_loop(2 * early, chans, bands, 0)
    remote(zrecv.at[1:], zrecv.at[1:], z_recv, z_recv, peer(1)).wait_recv()

    zrows[...] = zrecv[...].astype(F32).reshape(ns * chans, tok)

    def convolve(c, carry):
        zpad[c, ns:] = zrows[pl.ds(c, ns, stride=chans), :]
        total = jnp.zeros((ns, 2 * tok), F32)
        for k in range(0, ns, 2):
            two = jnp.concatenate((zpad[c, ns - k : 2 * ns - k], zpad[c, ns - k - 1 : 2 * ns - k - 1]), axis=1).astype(BF16)
            total += jnp.dot(two, toep[c, k * tok : (k + 2) * tok, :], preferred_element_type=F32)
        crows[pl.ds(c, ns, stride=chans), :] = total[:, :tok] + total[:, tok:]
        return carry

    lax.fori_loop(0, chans, convolve, 0)
    csend[...] = crows[...].astype(BF16).reshape(ns, chans, tok)
    crecv[s] = csend[s]

    def send_conv(i, carry):
        remote(csend.at[peer(i)], crecv.at[s], c_send, c_recv, peer(i)).start()
        return carry

    lax.fori_loop(1, ns, send_conv, 0)
    ext[1, 0:tok] = short(0)
    remote(zsend.at[1:], zsend.at[1:], z_send, z_send, peer(1)).wait_send()
    remote(crecv.at[1:], crecv.at[1:], c_recv, c_recv, peer(1)).wait_recv()
    conv = crecv[...].astype(F32).reshape(ns * chans, tok).T
    out_ref[...] = (res_ref[...].astype(F32) + ext[1, 0:tok] * conv).astype(BF16)
    remote(csend.at[1:], csend.at[1:], c_send, c_send, peer(1)).wait_send()


def mixer(residual, query, key, value, short_kernel, raw, decay):
    ns = lax.axis_size("seq")
    tok, width = query.shape
    tap_count = short_kernel.shape[1]
    chans, length = raw.shape
    root = jnp.sqrt(jnp.expm1(-2.0 * decay * length) / jnp.expm1(-2.0 * decay))
    vmem, dma = pltpu.VMEM, pltpu.SemaphoreType.DMA
    return pl.pallas_call(
        functools.partial(mixer_kernel, (ns, tok, chans, tap_count)),
        out_shape=jax.ShapeDtypeStruct((tok, width), BF16),
        in_specs=[pl.BlockSpec(memory_space=pltpu.VMEM)] * 8,
        out_specs=pl.BlockSpec(memory_space=pltpu.VMEM),
        scratch_shapes=[
            vmem((3, 8 + tok, width), F32),
            vmem((3, 16, width), BF16),
            vmem((3, 16, width), BF16),
            vmem((chans, 8, length), F32),
            vmem((chans, length, 2 * tok), BF16),
            vmem((ns, chans, tok), BF16),
            vmem((ns, chans, tok), BF16),
            vmem((ns * chans, tok), F32),
            vmem((chans, 2 * ns, tok), F32),
            vmem((ns * chans, tok), F32),
            vmem((ns, chans, tok), BF16),
            vmem((ns, chans, tok), BF16),
        ] + [pltpu.SemaphoreType.DMA] * 6,
        compiler_params=pltpu.CompilerParams(
            collective_id=0, has_side_effects=True, vmem_limit_bytes=56 * 1024 * 1024
        ),
    )(residual, query, key, value, short_kernel, raw, decay, root)


def expert_kernel(
    dims,
    mixed_ref, place_ref, wmap_ref, gain_ref, wg_hbm, wu_hbm, wd_hbm, out_ref,
    wg, wu, wd, outg, arr, xa, xb, acc_g, acc_u, hid, pc, pd, rc1, rc2, rd1, rd2, yb, ret,
    w_sem, go_send, go_recv, a_recv, b_recv, rc1_recv, rc2_recv, rd1_recv, rd2_recv, back_send, back_recv,
    az_send, ax_send, bz_send, bx_send, cz_send, cx_send, dz_send, dx_send,
):
    nz, nx, ne, cap, wa, wb = dims
    width = 2 * (wa + wb)
    chunk = width // ne
    s, e = lax.axis_index("seq"), lax.axis_index("exp")
    z, x = s // nx, s % nx

    def along_z(d):
        return (((z + (1, nz - 1)[d]) % nz) * nx + x, e)

    def along_x(d):
        return (z * nx + (x + (1, nx - 1)[d]) % nx, e)

    def expert(i):
        return (s, (e + i) % ne)

    def remote(src, dst, send, recv, to):
        return pltpu.make_async_remote_copy(
            src_ref=src, dst_ref=dst, send_sem=send, recv_sem=recv, device_id=to, device_id_type=MESH
        )

    def arrived(dst, recv):
        remote(dst, dst, recv, recv, along_z(0)).wait_recv()

    def sent(src, send):
        remote(src, src, send, send, along_z(0)).wait_send()

    weights = [
        pltpu.make_async_copy(h.at[0], v, w_sem.at[i]) for i, (h, v) in enumerate(((wg_hbm, wg), (wu_hbm, wu), (wd_hbm, wd)))
    ]
    for copy in weights:
        copy.start()

    barrier = pltpu.get_barrier_semaphore()
    partners = [along_z(0), along_z(1), along_x(0), along_x(1)] + [expert(i) for i in range(1, ne)]
    for to in partners:
        pl.semaphore_signal(barrier, inc=1, device_id=to, device_id_type=MESH)
    picked = jnp.dot(place_ref[...], mixed_ref[...], preferred_element_type=F32)
    outg[...] = picked.reshape(ne, cap, chunk).astype(BF16)
    arr[e] = outg[e]
    acc_g[...] = jnp.zeros_like(acc_g)
    acc_u[...] = jnp.zeros_like(acc_u)
    pl.semaphore_wait(barrier, len(partners))

    for i in range(1, ne):
        remote(outg.at[(e + i) % ne], arr.at[e], go_send.at[i], go_recv.at[i], expert(i)).start()
    for i in range(1, ne):
        arrived(arr.at[(e + ne - i) % ne], go_recv.at[i])
    square = jnp.zeros((cap, 1), F32)
    for c in range(ne):
        values = arr[c].astype(F32)
        square += jnp.sum(values * values, axis=-1, keepdims=True)
    scale = lax.rsqrt(square / width + 1e-06)
    spans = []
    for d in range(2):
        spans.append((xa, pc, d, d * wa, wa))
        spans.append((xb, pd, d, 2 * wa + d * wb, wb))
    for c in range(ne):
        values = (arr[c].astype(F32) * scale * gain_ref[:, c * chunk : (c + 1) * chunk]).astype(BF16)
        for ref, _, d, start, size in spans:
            lo, hi = max(start, c * chunk), min(start + size, (c + 1) * chunk)
            if lo < hi:
                ref[d, 0, 0, :, lo - start : hi - start] = values[:, lo - c * chunk : hi - c * chunk]

    def a_along_z(d, t, j):
        remote(xa.at[d, t, j], xa.at[d, t + 1, j], az_send.at[d], a_recv.at[d, t + 1, j], along_z(d)).start()

    def a_along_x(d, j):
        remote(xa.at[d, 0, j], xa.at[d, 0, j + 1], ax_send.at[d], a_recv.at[d, 0, j + 1], along_x(d)).start()

    def b_along_z(d, t):
        remote(xb.at[d, t, 0], xb.at[d, t + 1, 0], bz_send.at[d], b_recv.at[d, t + 1, 0], along_z(d)).start()

    def b_along_x(d, t, j):
        remote(xb.at[d, t, j], xb.at[d, t, j + 1], bx_send.at[d], b_recv.at[d, t, j + 1], along_x(d)).start()

    for d in range(2):
        b_along_z(d, 0)
        a_along_x(d, 0)
    for d in range(2):
        b_along_x(d, 0, 0)
        a_along_z(d, 0, 0)

    def turned(j, d):
        return (nx - j) % nx if d else j

    def rows_of(ref, d, t):
        parts = [ref[d, t, turned(j, d)].astype(F32) for j in range(nx)]
        return jnp.concatenate(parts, axis=0).astype(BF16)

    def group(d, t):
        return (nz - t) % nz if d else t

    def across(rows, w):
        return lax.dot_general(rows, w, (((1,), (1,)), ((), ())), preferred_element_type=F32)

    def project(d, t):
        at = group(d, t)
        left, right = rows_of(xa, d, t), rows_of(xb, d, t)
        one = slice(d * wa, (d + 1) * wa)
        two = slice(2 * wa + d * wb, 2 * wa + (d + 1) * wb)
        for total, w in ((acc_g, wg), (acc_u, wu)):
            total[at] += across(left, w[:, one]) + across(right, w[:, two])

    def activate(d, t):
        at = group(d, t)
        gate = acc_g[at]
        hid[at] = (gate / (1.0 + jnp.exp(-gate)) * acc_u[at]).astype(BF16)

    def gather_step(p, carry):
        for d in range(2):
            @pl.when(p <= nz - 1)
            def _():
                arrived(xb.at[d, p, 0], b_recv.at[d, p, 0])
                b_along_x(d, p, 0)

            @pl.when(p < nz - 1)
            def _():
                b_along_z(d, p)

            @pl.when(p <= nx - 1)
            def _():
                arrived(xa.at[d, 0, p], a_recv.at[d, 0, p])
                a_along_z(d, 0, p)

            @pl.when(p < nx - 1)
            def _():
                a_along_x(d, p)

        for j in range(nx):
            for d in range(2):
                t = p - j

                @pl.when((t >= 1) & (t <= nz - 1))
                def _():
                    arrived(xa.at[d, t, j], a_recv.at[d, t, j])

                @pl.when((t >= 1) & (t < nz - 1))
                def _():
                    a_along_z(d, t, j)

            if j >= 1:
                for d in range(2):
                    t = p - j

                    @pl.when((t >= 0) & (t <= nz - 1))
                    def _():
                        arrived(xb.at[d, t, j], b_recv.at[d, t, j])
                        if j < nx - 1:
                            b_along_x(d, t, j)

        @pl.when(p == nx - 1)
        def _():
            for copy in weights:
                copy.wait()

        for d in range(2):
            t = p - (nx - 1)

            @pl.when(t >= 0)
            def _():
                project(d, t)

            @pl.when((t > nz // 2) | ((t == 0) | (t == nz // 2)) & (d == 1))
            def _():
                activate(d, t)

        return carry

    lax.fori_loop(1, nz + nx - 1, gather_step, 0)

    def down(d, q):
        at = group(d, q % nz)
        rows = hid[at]
        for ref, start, size in ((pc, d * wa, wa), (pd, 2 * wa + d * wb, wb)):
            part = jnp.dot(rows, wd[:, start : start + size], preferred_element_type=F32)
            for j in range(nx):
                ref[d, q - 1, turned(j, d)] = part[j * cap : (j + 1) * cap].astype(BF16)

    def add(total, more):
        total[...] = (total[...].astype(F32) + more[...].astype(F32)).astype(BF16)

    for d in range(2):
        down(d, 1)

    def reduce_step(p, carry):
        for d in range(2):
            for v in range(1, nx + 1):
                k, j = p - v + 1, v % nx

                @pl.when((k >= 1) & (k <= nz))
                def _():
                    if v >= 2:
                        arrived(rd1.at[d, v - 2, k - 1], rd1_recv.at[d, v - 2, k - 1])
                        add(pd.at[d, k - 1, j], rd1.at[d, v - 2, k - 1])
                    if v < nx:
                        remote(
                            pd.at[d, k - 1, j], rd1.at[d, v - 1, k - 1], dx_send.at[d], rd1_recv.at[d, v - 1, k - 1], along_x(d)
                        ).start()
                    else:
                        @pl.when(k >= 2)
                        def _():
                            arrived(rd2.at[d, k - 2], rd2_recv.at[d, k - 2])
                            add(pd.at[d, k - 1, 0], rd2.at[d, k - 2])

                        @pl.when(k < nz)
                        def _():
                            remote(
                                pd.at[d, k - 1, 0], rd2.at[d, k - 1], dz_send.at[d], rd2_recv.at[d, k - 1], along_z(d)
                            ).start()

        for d in range(2):
            for v in range(1, nx + 1):
                q, j = p - v + 1, v % nx

                @pl.when((q >= 2) & (q <= nz))
                def _():
                    arrived(rc1.at[d, q - 2, j], rc1_recv.at[d, q - 2, j])
                    add(pc.at[d, q - 1, j], rc1.at[d, q - 2, j])

                @pl.when((q >= 1) & (q < nz))
                def _():
                    remote(
                        pc.at[d, q - 1, j], rc1.at[d, q - 1, j], cz_send.at[d], rc1_recv.at[d, q - 1, j], along_z(d)
                    ).start()

                @pl.when(q == nz)
                def _():
                    if v >= 2:
                        arrived(rc2.at[d, v - 2], rc2_recv.at[d, v - 2])
                        add(pc.at[d, nz - 1, j], rc2.at[d, v - 2])
                    if v < nx:
                        remote(
                            pc.at[d, nz - 1, j], rc2.at[d, v - 1], cx_send.at[d], rc2_recv.at[d, v - 1], along_x(d)
                        ).start()

        for d in range(2):
            @pl.when(p < nz)
            def _():
                down(d, p + 1)

        return carry

    lax.fori_loop(1, nz + nx, reduce_step, 0)

    for c in range(ne):
        for _, ref, d, start, size in spans:
            lo, hi = max(start, c * chunk), min(start + size, (c + 1) * chunk)
            if lo < hi:
                yb[c, :, lo - c * chunk : hi - c * chunk] = ref[d, nz - 1, 0, :, lo - start : hi - start]
    for i in range(1, ne):
        remote(yb.at[(e + i) % ne], ret.at[e], back_send.at[i], back_recv.at[i], expert(i)).start()
    ret[e] = yb[e]
    for d in range(2):
        sent(xa.at[d, 0 : nz - 1], az_send.at[d])
        sent(xa.at[d, 0, 0 : nx - 1], ax_send.at[d])
        sent(xb.at[d, 0 : nz - 1, 0], bz_send.at[d])
        sent(xb.at[d, :, 0 : nx - 1], bx_send.at[d])
        sent(pc.at[d, 0 : nz - 1], cz_send.at[d])
        sent(pc.at[d, nz - 1, 0 : nx - 1], cx_send.at[d])
        sent(pd.at[d, 0 : nz - 1, 0], dz_send.at[d])
        sent(pd.at[d, :, 0 : nx - 1], dx_send.at[d])
    for i in range(1, ne):
        sent(outg.at[i], go_send.at[i])
    for i in range(1, ne):
        arrived(ret.at[(e + ne - i) % ne], back_recv.at[i])
    rows = ret[...].astype(F32).reshape(ne * cap, chunk)
    combined = jnp.dot(wmap_ref[...], rows, preferred_element_type=F32, precision=lax.Precision.HIGHEST)
    out_ref[...] = (mixed_ref[...].astype(F32) + combined).astype(BF16)
    for i in range(1, ne):
        sent(yb.at[i], back_send.at[i])


def experts(mixed, place, wmap, gain, w_gate, w_up, w_down, nz, nx, parts):
    ne = lax.axis_size("exp")
    cap = place.shape[0] // ne
    chunk = mixed.shape[1]
    width = ne * chunk
    wa, wb = parts
    hidden = w_gate.shape[2]
    vmem, dma = pltpu.VMEM, pltpu.SemaphoreType.DMA
    scratch = [
        vmem((hidden, width), BF16),
        vmem((hidden, width), BF16),
        vmem((hidden, width), BF16),
        vmem((ne, cap, chunk), BF16),
        vmem((ne, cap, chunk), BF16),
        vmem((2, nz, nx, cap, wa), BF16),
        vmem((2, nz, nx, cap, wb), BF16),
        vmem((nz, nx * cap, hidden), F32),
        vmem((nz, nx * cap, hidden), F32),
        vmem((nz, nx * cap, hidden), BF16),
        vmem((2, nz, nx, cap, wa), BF16),
        vmem((2, nz, nx, cap, wb), BF16),
        vmem((2, nz - 1, nx, cap, wa), BF16),
        vmem((2, nx - 1, cap, wa), BF16),
        vmem((2, nx - 1, nz, cap, wb), BF16),
        vmem((2, nz - 1, cap, wb), BF16),
        vmem((ne, cap, chunk), BF16),
        vmem((ne, cap, chunk), BF16),
        dma((3,)),
        dma((ne,)),
        dma((ne,)),
        dma((2, nz, nx)),
        dma((2, nz, nx)),
        dma((2, nz - 1, nx)),
        dma((2, nx - 1)),
        dma((2, nx - 1, nz)),
        dma((2, nz - 1)),
        dma((ne,)),
        dma((ne,)),
    ] + [dma((2,))] * 8
    return pl.pallas_call(
        functools.partial(expert_kernel, (nz, nx, ne, cap, wa, wb)),
        out_shape=jax.ShapeDtypeStruct(mixed.shape, BF16),
        in_specs=[pl.BlockSpec(memory_space=pltpu.VMEM)] * 4 + [pl.BlockSpec(memory_space=pl.ANY)] * 3,
        out_specs=pl.BlockSpec(memory_space=pltpu.VMEM),
        scratch_shapes=scratch,
        compiler_params=pltpu.CompilerParams(
            collective_id=1, has_side_effects=True, vmem_limit_bytes=60 * 1024 * 1024
        ),
    )(mixed, place, wmap, gain, jnp.swapaxes(w_gate, 1, 2), jnp.swapaxes(w_up, 1, 2), w_down)


def slot_keys(routes, expert_count, capacity):
    tokens = routes.shape[0]
    hot = (routes[:, :, None] == jnp.arange(expert_count, dtype=jnp.int32)).astype(F32)
    before = (jnp.arange(tokens)[:, None] > jnp.arange(tokens)[None, :]).astype(F32)
    earlier = jnp.dot(before, jnp.sum(hot, axis=1))
    slot = jnp.sum(hot * earlier[:, None, :], axis=2).astype(jnp.int32)
    return routes * capacity + slot


def slot_maps(routes, gate_weights, expert_count, capacity):
    keys = slot_keys(routes, expert_count, capacity)
    rows = jnp.arange(expert_count * capacity, dtype=jnp.int32)
    place = ((keys[None, :, 0] == rows[:, None]) | (keys[None, :, 1] == rows[:, None])).astype(BF16)
    wmap = sum(jnp.where(keys[:, k, None] == rows[None, :], gate_weights[:, k, None], 0.0) for k in range(2))
    return place, wmap


def on_device(
    residual,
    query_proj,
    key_proj,
    value_proj,
    short_kernel,
    filter_raw,
    filter_decay,
    routes,
    gate_weights,
    norm_gain,
    w_gate,
    w_up,
    w_down,
):
    tokens = query_proj.shape[0]
    nz, nx = lax.axis_size("seq") // 4, 4
    mixed = mixer(
        residual,
        query_proj,
        key_proj,
        value_proj,
        short_kernel,
        filter_raw[:, 0, :].T,
        filter_decay.T,
    )
    expert_total = lax.axis_size("exp")
    capacity = 5 * tokens * routes.shape[1] // (4 * expert_total)
    place, wmap = slot_maps(routes, gate_weights, expert_total, capacity)
    return experts(mixed, place, wmap, norm_gain[None, :], w_gate, w_up, w_down, nz, nx, (768, 1280))


def solution(mesh):
    in_specs = (
        P("seq", "exp"),
        P("seq", "exp"),
        P("seq", "exp"),
        P("seq", "exp"),
        P(None, None, "exp"),
        P(None, "exp", "seq"),
        P("exp", "seq"),
        P("seq", None),
        P("seq", None),
        P(),
        P("exp", None, "seq"),
        P("exp", None, "seq"),
        P("exp", "seq", None),
    )
    out_specs = P("seq", "exp")
    return jax.shard_map(
        on_device, mesh=mesh, in_specs=in_specs, out_specs=out_specs, check_vma=False
    )
```

```python
import functools

import jax
import jax.numpy as jnp
from jax import lax
from jax.experimental import pallas as pl
from jax.experimental.pallas import tpu as pltpu
from jax.sharding import PartitionSpec as P

MESH = pl.DeviceIdType.MESH
F32, BF16 = jnp.float32, jnp.bfloat16


def column(row):
    n = row.shape[1]
    same = lax.broadcasted_iota(jnp.int32, (n, n), 0) == lax.broadcasted_iota(jnp.int32, (n, n), 1)
    return jnp.sum(jnp.where(same, jnp.broadcast_to(row, (n, n)), 0.0), axis=1, keepdims=True)


def less_one(v):
    series = jnp.ones_like(v)
    for n in range(11, 1, -1):
        series = 1.0 + v * (1.0 / n) * series
    return jnp.where(v > -0.5, v * series, jnp.exp(v) - 1.0)


def slot_maps(routes_ref, picks_ref, place, wmap, ne, cap):
    topk, tok = routes_ref.shape
    routes = routes_ref[...]
    ids = lax.broadcasted_iota(jnp.int32, (ne, tok), 0)
    hot = [(ids == routes[k : k + 1]).astype(F32) for k in range(topk)]
    before = lax.broadcasted_iota(jnp.int32, (tok, tok), 0) < lax.broadcasted_iota(jnp.int32, (tok, tok), 1)
    earlier = jnp.dot(sum(hot).astype(BF16), before.astype(F32).astype(BF16), preferred_element_type=F32)
    row = lax.broadcasted_iota(jnp.int32, (ne * cap, tok), 0).astype(F32)
    marks, weights = 0.0, 0.0
    for k in range(topk):
        key = routes[k : k + 1].astype(F32) * cap + jnp.sum(hot[k] * earlier, axis=0, keepdims=True)
        marks += jnp.where(row == key, 1.0, 0.0)
        weights += jnp.where(row == key, picks_ref[k : k + 1, :], 0.0)
    place[...] = marks.astype(BF16)
    wmap[...] = weights


def block_kernel(
    dims,
    res_ref, q_ref, k_ref, v_ref, filt_ref, raw_ref, decay_ref, routes_ref, picks_ref, gain_ref, wg_hbm, wu_hbm, wd_hbm,
    out_ref,
    mixed, place, wmap, ext, rims, edge, zsend, zrecv, csend, crecv,
    wg, wu, wd, outg, arr, xa, xb, rc1, rc2, rd1, rd2, yb, ret,
    rim_send, rim_recv, z_send, z_recv, c_send, c_recv,
    w_sem, go_send, go_recv, a_recv, b_recv, rc1_recv, rc2_recv, rd1_recv, rd2_recv, back_send, back_recv,
    az_send, ax_send, bz_send, bx_send, cz_send, cx_send, dz_send, dx_send,
):
    nz, nx, ne, cap, wa, wb = dims
    width = 2 * (wa + wb)
    chunk = width // ne
    ns, tok = nz * nx, q_ref.shape[0]
    chans, length = raw_ref.shape
    rim = rims.shape[1]
    s, e = lax.axis_index("seq"), lax.axis_index("exp")
    z, x = s // nx, s % nx

    def peer(i):
        return (s + i) % ns

    def along_z(d):
        return (((z + (1, nz - 1)[d]) % nz) * nx + x, e)

    def along_x(d):
        return (z * nx + (x + (1, nx - 1)[d]) % nx, e)

    def expert(i):
        return (s, (e + i) % ne)

    def remote(src, dst, send, recv, to):
        return pltpu.make_async_remote_copy(
            src_ref=src, dst_ref=dst, send_sem=send, recv_sem=recv, device_id=to, device_id_type=MESH
        )

    def arrived(dst, recv):
        remote(dst, dst, recv, recv, along_z(0)).wait_recv()

    def sent(src, send):
        remote(src, src, send, send, along_z(0)).wait_send()

    weights = [
        pltpu.make_async_copy(h.at[0], v, w_sem.at[i]) for i, (h, v) in enumerate(((wg_hbm, wg), (wu_hbm, wu), (wd_hbm, wd)))
    ]
    for copy in weights:
        copy.start()

    barrier = pltpu.get_barrier_semaphore()

    def greet(i, carry):
        pl.semaphore_signal(barrier, inc=1, device_id=(peer(i), e), device_id_type=MESH)
        return carry

    lax.fori_loop(1, ns, greet, 0)
    for i in range(1, ne):
        pl.semaphore_signal(barrier, inc=1, device_id=expert(i), device_id_type=MESH)

    def mixer(taps, toep, zrows, zpad, crows):
        for j, ref in enumerate((q_ref, k_ref, v_ref)):
            edge[j] = ref[tok - rim :, :]
            ext[j, 8 : 8 + tok] = ref[...].astype(F32)
        zpad[...] = jnp.zeros_like(zpad)
        position = lax.broadcasted_iota(jnp.int32, (chans, length), 1).astype(F32)
        decay = column(decay_ref[...])
        root = jnp.sqrt(less_one(-2.0 * decay * length) / less_one(-2.0 * decay))
        scaled = raw_ref[...] * jnp.exp(-decay * position) / root
        for c in range(chans):
            taps[c] = jnp.broadcast_to(scaled[c : c + 1, :], (8, length))

        band = lax.broadcasted_iota(jnp.int32, (tok, tok), 1) >= lax.broadcasted_iota(jnp.int32, (tok, tok), 0)

        def bands(c, carry):
            before = jnp.zeros((tok, tok), F32)
            for k in range(ns):
                row = jnp.concatenate([taps[c, :, k * tok : (k + 1) * tok]] * (tok // 8), axis=0)
                turned = pltpu.roll(row, 0, axis=1, stride=1, stride_axis=0)
                full = jnp.where(band, turned, before)
                toep[c, k * tok : (k + 1) * tok, :] = full.astype(BF16)
                before = turned
            return carry

        early = chans // 4
        lax.fori_loop(0, early, bands, 0)
        slot_maps(routes_ref, picks_ref, place, wmap, ne, cap)
        pl.semaphore_wait(barrier, ns - 1 + ne - 1)

        rim_copy = remote(edge, rims, rim_send, rim_recv, (peer(1), e))
        rim_copy.start()
        lax.fori_loop(early, 2 * early, bands, 0)
        rim_copy.wait()

        def short(j):
            return (
                filt_ref[j, 0:1, :] * ext[j, 8 : 8 + tok]
                + filt_ref[j, 1:2, :] * ext[j, 7 : 7 + tok]
                + filt_ref[j, 2:3, :] * ext[j, 6 : 6 + tok]
            )

        for j in range(3):
            ext[j, 0:8] = jnp.where(s == 0, 0.0, rims[j].astype(F32)[rim - 8 :])
        zed = (short(1) * short(2)).astype(BF16).astype(F32)
        zsend[...] = zed.T.astype(BF16).reshape(ns, chans, tok)
        zrecv[s] = zsend[s]

        def send_zed(i, carry):
            remote(zsend.at[peer(i)], zrecv.at[s], z_send, z_recv, (peer(i), e)).start()
            return carry

        lax.fori_loop(1, ns, send_zed, 0)
        lax.fori_loop(2 * early, chans, bands, 0)
        remote(zrecv.at[1:], zrecv.at[1:], z_recv, z_recv, (peer(1), e)).wait_recv()

        zrows[...] = zrecv[...].astype(F32).reshape(ns * chans, tok)

        def convolve(c):
            zpad[c, ns:] = zrows[pl.ds(c, ns, stride=chans), :]
            total = jnp.zeros((ns, tok), F32)
            for k in range(0, ns, 2):
                two = jnp.concatenate((zpad[c, ns - k : 2 * ns - k], zpad[c, ns - k - 1 : 2 * ns - k - 1]), axis=1).astype(BF16)
                total += jnp.dot(two, toep[c, k * tok : (k + 2) * tok, :], preferred_element_type=F32)
            crows[pl.ds(c, ns, stride=chans), :] = total

        def convolve_some(g, carry):
            for c in range(chans // 4):
                convolve(g * (chans // 4) + c)
            return carry

        lax.fori_loop(0, 4, convolve_some, 0)
        csend[...] = crows[...].astype(BF16).reshape(ns, chans, tok)
        crecv[s] = csend[s]

        def send_conv(i, carry):
            remote(csend.at[peer(i)], crecv.at[s], c_send, c_recv, (peer(i), e)).start()
            return carry

        lax.fori_loop(1, ns, send_conv, 0)
        ext[1, 0:tok] = short(0)
        remote(zsend.at[1:], zsend.at[1:], z_send, z_send, (peer(1), e)).wait_send()
        remote(crecv.at[1:], crecv.at[1:], c_recv, c_recv, (peer(1), e)).wait_recv()
        conv = crecv[...].astype(F32).reshape(ns * chans, tok).T
        mixed[...] = (res_ref[...].astype(F32) + ext[1, 0:tok] * conv).astype(BF16)
        remote(csend.at[1:], csend.at[1:], c_send, c_send, (peer(1), e)).wait_send()

    vmem = pltpu.VMEM
    pl.run_scoped(
        mixer,
        vmem((chans, 8, length), F32),
        vmem((chans, length, tok), BF16),
        vmem((ns * chans, tok), F32),
        vmem((chans, 2 * ns, tok), F32),
        vmem((ns * chans, tok), F32),
    )

    def experts(acc_g, acc_u, hid, pc, pd):
        picked = jnp.dot(place[...], mixed[...], preferred_element_type=F32)
        outg[...] = picked.reshape(ne, cap, chunk).astype(BF16)
        arr[e] = outg[e]
        for i in range(1, ne):
            remote(outg.at[(e + i) % ne], arr.at[e], go_send.at[i], go_recv.at[i], expert(i)).start()
        acc_g[...] = jnp.zeros_like(acc_g)
        acc_u[...] = jnp.zeros_like(acc_u)
        for i in range(1, ne):
            arrived(arr.at[(e + ne - i) % ne], go_recv.at[i])
        square = jnp.zeros((cap, 1), F32)
        for c in range(ne):
            values = arr[c].astype(F32)
            square += jnp.sum(values * values, axis=-1, keepdims=True)
        scale = lax.rsqrt(square / width + 1e-06)
        spans = []
        for d in range(2):
            spans.append((xa, pc, d, d * wa, wa))
            spans.append((xb, pd, d, 2 * wa + d * wb, wb))
        for c in range(ne):
            values = (arr[c].astype(F32) * scale * gain_ref[:, c * chunk : (c + 1) * chunk]).astype(BF16)
            for ref, _, d, start, size in spans:
                lo, hi = max(start, c * chunk), min(start + size, (c + 1) * chunk)
                if lo < hi:
                    ref[d, 0, 0, :, lo - start : hi - start] = values[:, lo - c * chunk : hi - c * chunk]

        def a_along_z(d, t, j):
            remote(xa.at[d, t, j], xa.at[d, t + 1, j], az_send.at[d], a_recv.at[d, t + 1, j], along_z(d)).start()

        def a_along_x(d, j):
            remote(xa.at[d, 0, j], xa.at[d, 0, j + 1], ax_send.at[d], a_recv.at[d, 0, j + 1], along_x(d)).start()

        def b_along_z(d, t):
            remote(xb.at[d, t, 0], xb.at[d, t + 1, 0], bz_send.at[d], b_recv.at[d, t + 1, 0], along_z(d)).start()

        def b_along_x(d, t, j):
            remote(xb.at[d, t, j], xb.at[d, t, j + 1], bx_send.at[d], b_recv.at[d, t, j + 1], along_x(d)).start()

        for d in range(2):
            b_along_z(d, 0)
            a_along_x(d, 0)
        for d in range(2):
            b_along_x(d, 0, 0)
            a_along_z(d, 0, 0)

        def turned(j, d):
            return (nx - j) % nx if d else j

        def rows_of(ref, d, t):
            parts = [ref[d, t, turned(j, d)].astype(F32) for j in range(nx)]
            return jnp.concatenate(parts, axis=0).astype(BF16)

        def group(d, t):
            return (nz - t) % nz if d else t

        def across(rows, w):
            return lax.dot_general(rows, w, (((1,), (1,)), ((), ())), preferred_element_type=F32)

        def project(d, t):
            at = group(d, t)
            left, right = rows_of(xa, d, t), rows_of(xb, d, t)
            one = slice(d * wa, (d + 1) * wa)
            two = slice(2 * wa + d * wb, 2 * wa + (d + 1) * wb)
            for total, w in ((acc_g, wg), (acc_u, wu)):
                total[at] += across(left, w[:, one]) + across(right, w[:, two])

        def activate(d, t):
            at = group(d, t)
            gate = acc_g[at]
            hid[at] = (gate / (1.0 + jnp.exp(-gate)) * acc_u[at]).astype(BF16)

        def gather_step(p, carry):
            for d in range(2):
                @pl.when(p <= nz - 1)
                def _():
                    arrived(xb.at[d, p, 0], b_recv.at[d, p, 0])
                    b_along_x(d, p, 0)

                @pl.when(p < nz - 1)
                def _():
                    b_along_z(d, p)

                @pl.when(p <= nx - 1)
                def _():
                    arrived(xa.at[d, 0, p], a_recv.at[d, 0, p])
                    a_along_z(d, 0, p)

                @pl.when(p < nx - 1)
                def _():
                    a_along_x(d, p)

            for j in range(nx):
                for d in range(2):
                    t = p - j

                    @pl.when((t >= 1) & (t <= nz - 1))
                    def _():
                        arrived(xa.at[d, t, j], a_recv.at[d, t, j])

                    @pl.when((t >= 1) & (t < nz - 1))
                    def _():
                        a_along_z(d, t, j)

                if j >= 1:
                    for d in range(2):
                        t = p - j

                        @pl.when((t >= 0) & (t <= nz - 1))
                        def _():
                            arrived(xb.at[d, t, j], b_recv.at[d, t, j])
                            if j < nx - 1:
                                b_along_x(d, t, j)

            @pl.when(p == nx - 1)
            def _():
                for copy in weights:
                    copy.wait()

            for d in range(2):
                t = p - (nx - 1)

                @pl.when(t >= 0)
                def _():
                    project(d, t)

                @pl.when((t > nz // 2) | ((t == 0) | (t == nz // 2)) & (d == 1))
                def _():
                    activate(d, t)

            return carry

        lax.fori_loop(1, nz + nx - 1, gather_step, 0)

        def down(d, q):
            at = group(d, q % nz)
            rows = hid[at]
            for ref, start, size in ((pc, d * wa, wa), (pd, 2 * wa + d * wb, wb)):
                part = jnp.dot(rows, wd[:, start : start + size], preferred_element_type=F32)
                for j in range(nx):
                    ref[d, q - 1, turned(j, d)] = part[j * cap : (j + 1) * cap].astype(BF16)

        def add(total, more):
            total[...] = (total[...].astype(F32) + more[...].astype(F32)).astype(BF16)

        for d in range(2):
            down(d, 1)

        def reduce_step(p, carry):
            for d in range(2):
                for v in range(1, nx + 1):
                    k, j = p - v + 1, v % nx

                    @pl.when((k >= 1) & (k <= nz))
                    def _():
                        if v >= 2:
                            arrived(rd1.at[d, v - 2, k - 1], rd1_recv.at[d, v - 2, k - 1])
                            add(pd.at[d, k - 1, j], rd1.at[d, v - 2, k - 1])
                        if v < nx:
                            remote(
                                pd.at[d, k - 1, j], rd1.at[d, v - 1, k - 1], dx_send.at[d], rd1_recv.at[d, v - 1, k - 1], along_x(d)
                            ).start()
                        else:
                            @pl.when(k >= 2)
                            def _():
                                arrived(rd2.at[d, k - 2], rd2_recv.at[d, k - 2])
                                add(pd.at[d, k - 1, 0], rd2.at[d, k - 2])

                            @pl.when(k < nz)
                            def _():
                                remote(
                                    pd.at[d, k - 1, 0], rd2.at[d, k - 1], dz_send.at[d], rd2_recv.at[d, k - 1], along_z(d)
                                ).start()

            for d in range(2):
                for v in range(1, nx + 1):
                    q, j = p - v + 1, v % nx

                    @pl.when((q >= 2) & (q <= nz))
                    def _():
                        arrived(rc1.at[d, q - 2, j], rc1_recv.at[d, q - 2, j])
                        add(pc.at[d, q - 1, j], rc1.at[d, q - 2, j])

                    @pl.when((q >= 1) & (q < nz))
                    def _():
                        remote(
                            pc.at[d, q - 1, j], rc1.at[d, q - 1, j], cz_send.at[d], rc1_recv.at[d, q - 1, j], along_z(d)
                        ).start()

                    @pl.when(q == nz)
                    def _():
                        if v >= 2:
                            arrived(rc2.at[d, v - 2], rc2_recv.at[d, v - 2])
                            add(pc.at[d, nz - 1, j], rc2.at[d, v - 2])
                        if v < nx:
                            remote(
                                pc.at[d, nz - 1, j], rc2.at[d, v - 1], cx_send.at[d], rc2_recv.at[d, v - 1], along_x(d)
                            ).start()

            for d in range(2):
                @pl.when(p < nz)
                def _():
                    down(d, p + 1)

            return carry

        lax.fori_loop(1, nz + nx, reduce_step, 0)

        for c in range(ne):
            for _, ref, d, start, size in spans:
                lo, hi = max(start, c * chunk), min(start + size, (c + 1) * chunk)
                if lo < hi:
                    yb[c, :, lo - c * chunk : hi - c * chunk] = ref[d, nz - 1, 0, :, lo - start : hi - start]
        for i in range(1, ne):
            remote(yb.at[(e + i) % ne], ret.at[e], back_send.at[i], back_recv.at[i], expert(i)).start()
        ret[e] = yb[e]
        for d in range(2):
            sent(xa.at[d, 0 : nz - 1], az_send.at[d])
            sent(xa.at[d, 0, 0 : nx - 1], ax_send.at[d])
            sent(xb.at[d, 0 : nz - 1, 0], bz_send.at[d])
            sent(xb.at[d, :, 0 : nx - 1], bx_send.at[d])
            sent(pc.at[d, 0 : nz - 1], cz_send.at[d])
            sent(pc.at[d, nz - 1, 0 : nx - 1], cx_send.at[d])
            sent(pd.at[d, 0 : nz - 1, 0], dz_send.at[d])
            sent(pd.at[d, :, 0 : nx - 1], dx_send.at[d])
        for i in range(1, ne):
            sent(outg.at[i], go_send.at[i])
        for i in range(1, ne):
            arrived(ret.at[(e + ne - i) % ne], back_recv.at[i])
        rows = ret[...].astype(F32).reshape(ne * cap, chunk)
        combined = lax.dot_general(
            wmap[...], rows, (((0,), (0,)), ((), ())), preferred_element_type=F32, precision=lax.Precision.HIGHEST
        )
        out_ref[...] = (mixed[...].astype(F32) + combined).astype(BF16)
        for i in range(1, ne):
            sent(yb.at[i], back_send.at[i])

    hidden = wd.shape[0]
    pl.run_scoped(
        experts,
        vmem((nz, nx * cap, hidden), F32),
        vmem((nz, nx * cap, hidden), F32),
        vmem((nz, nx * cap, hidden), BF16),
        vmem((2, nz, nx, cap, wa), BF16),
        vmem((2, nz, nx, cap, wb), BF16),
    )


def block(residual, query, key, value, short_kernel, raw, decay, routes, picks, gain, w_gate, w_up, w_down, nz, nx, parts):
    ns, ne = nz * nx, lax.axis_size("exp")
    tok, chunk = query.shape
    chans, length = raw.shape
    cap = 5 * tok * routes.shape[0] // (4 * ne)
    width = ne * chunk
    wa, wb = parts
    hidden = w_gate.shape[1]
    vmem, dma = pltpu.VMEM, pltpu.SemaphoreType.DMA
    scratch = [
        vmem((tok, chunk), BF16),
        vmem((ne * cap, tok), BF16),
        vmem((ne * cap, tok), F32),
        vmem((3, 8 + tok, chunk), F32),
        vmem((3, 16, chunk), BF16),
        vmem((3, 16, chunk), BF16),
    ]
    scratch += [vmem((ns, chans, tok), BF16)] * 4
    scratch += [vmem((hidden, width), BF16)] * 3
    scratch += [
        vmem((ne, cap, chunk), BF16),
        vmem((ne, cap, chunk), BF16),
        vmem((2, nz, nx, cap, wa), BF16),
        vmem((2, nz, nx, cap, wb), BF16),
        vmem((2, nz - 1, nx, cap, wa), BF16),
        vmem((2, nx - 1, cap, wa), BF16),
        vmem((2, nx - 1, nz, cap, wb), BF16),
        vmem((2, nz - 1, cap, wb), BF16),
        vmem((ne, cap, chunk), BF16),
        vmem((ne, cap, chunk), BF16),
    ]
    scratch += [dma] * 6
    scratch += [
        dma((3,)),
        dma((ne,)),
        dma((ne,)),
        dma((2, nz, nx)),
        dma((2, nz, nx)),
        dma((2, nz - 1, nx)),
        dma((2, nx - 1)),
        dma((2, nx - 1, nz)),
        dma((2, nz - 1)),
        dma((ne,)),
        dma((ne,)),
    ] + [dma((2,))] * 8
    return pl.pallas_call(
        functools.partial(block_kernel, (nz, nx, ne, cap, wa, wb)),
        out_shape=jax.ShapeDtypeStruct((tok, chunk), BF16),
        in_specs=[pl.BlockSpec(memory_space=pltpu.VMEM)] * 10 + [pl.BlockSpec(memory_space=pl.ANY)] * 3,
        out_specs=pl.BlockSpec(memory_space=pltpu.VMEM),
        scratch_shapes=scratch,
        compiler_params=pltpu.CompilerParams(
            collective_id=0, has_side_effects=True, vmem_limit_bytes=61 * 1024 * 1024
        ),
    )(residual, query, key, value, short_kernel, raw, decay, routes, picks, gain, w_gate, w_up, w_down)


def on_device(
    residual,
    query_proj,
    key_proj,
    value_proj,
    short_kernel,
    filter_raw,
    filter_decay,
    routes,
    gate_weights,
    norm_gain,
    w_gate,
    w_up,
    w_down,
):
    return block(
        residual,
        query_proj,
        key_proj,
        value_proj,
        short_kernel,
        filter_raw[:, 0, :].T,
        filter_decay,
        routes.T,
        gate_weights.T,
        norm_gain[None, :],
        jnp.swapaxes(w_gate, 1, 2),
        jnp.swapaxes(w_up, 1, 2),
        w_down,
        lax.axis_size("seq") // 4,
        4,
        (768, 1280),
    )


def solution(mesh):
    in_specs = (
        P("seq", "exp"),
        P("seq", "exp"),
        P("seq", "exp"),
        P("seq", "exp"),
        P(None, None, "exp"),
        P(None, "exp", "seq"),
        P("exp", "seq"),
        P("seq", None),
        P("seq", None),
        P(),
        P("exp", None, "seq"),
        P("exp", None, "seq"),
        P("exp", "seq", None),
    )
    out_specs = P("seq", "exp")
    return jax.shard_map(
        on_device, mesh=mesh, in_specs=in_specs, out_specs=out_specs, check_vma=False
    )
```

```python
import functools

import jax
import jax.numpy as jnp
from jax import lax
from jax.experimental import pallas as pl
from jax.experimental.pallas import tpu as pltpu
from jax.sharding import PartitionSpec as P

MESH = pl.DeviceIdType.MESH
F32, BF16 = jnp.float32, jnp.bfloat16


def column(row):
    n = row.shape[1]
    same = lax.broadcasted_iota(jnp.int32, (n, n), 0) == lax.broadcasted_iota(jnp.int32, (n, n), 1)
    return jnp.sum(jnp.where(same, jnp.broadcast_to(row, (n, n)), 0.0), axis=1, keepdims=True)


def less_one(v):
    series = jnp.ones_like(v)
    for n in range(11, 1, -1):
        series = 1.0 + v * (1.0 / n) * series
    return jnp.where(v > -0.5, v * series, jnp.exp(v) - 1.0)


def slot_maps(routes_ref, picks_ref, place, wmap, ne, cap):
    topk, tok = routes_ref.shape
    routes = routes_ref[...]
    ids = lax.broadcasted_iota(jnp.int32, (ne, tok), 0)
    hot = [(ids == routes[k : k + 1]).astype(F32) for k in range(topk)]
    before = lax.broadcasted_iota(jnp.int32, (tok, tok), 0) < lax.broadcasted_iota(jnp.int32, (tok, tok), 1)
    earlier = jnp.dot(sum(hot).astype(BF16), before.astype(F32).astype(BF16), preferred_element_type=F32)
    row = lax.broadcasted_iota(jnp.int32, (ne * cap, tok), 0).astype(F32)
    marks, weights = 0.0, 0.0
    for k in range(topk):
        key = routes[k : k + 1].astype(F32) * cap + jnp.sum(hot[k] * earlier, axis=0, keepdims=True)
        marks += jnp.where(row == key, 1.0, 0.0)
        weights += jnp.where(row == key, picks_ref[k : k + 1, :], 0.0)
    place[...] = marks.astype(BF16)
    wmap[...] = weights


def block_kernel(
    dims,
    res_ref, q_ref, k_ref, v_ref, filt_ref, raw_ref, decay_ref, routes_ref, picks_ref, gain_ref, wg_hbm, wu_hbm, wd_hbm,
    out_ref,
    mixed, place, wmap, ext, rims, edge, zsend, zrecv, csend, crecv,
    wg, wu, wd, outg, arr, xa, xb, rc1, rc2, rd1, rd2, yb, ret,
    rim_send, rim_recv, z_send, z_recv, c_send, c_recv,
    w_sem, go_send, go_recv, a_recv, b_recv, rc1_recv, rc2_recv, rd1_recv, rd2_recv, back_send, back_recv,
    az_send, ax_send, bz_send, bx_send, cz_send, cx_send, dz_send, dx_send,
):
    nz, nx, ne, cap, wa, wb = dims
    width = 2 * (wa + wb)
    chunk = width // ne
    ns, tok = nz * nx, q_ref.shape[0]
    chans, length = raw_ref.shape
    s, e = lax.axis_index("seq"), lax.axis_index("exp")
    z, x = s // nx, s % nx

    def peer(i):
        return (z + i // nx) % nz * nx + (x + i % nx) % nx

    def hops(i):
        return min(i // nx, nz - i // nx) + min(i % nx, nx - i % nx)

    far_first = sorted(range(1, ns), key=lambda i: -hops(i))
    chips = ne // 2

    def owner(i, way):
        return (e // 2 + (i // 2 if way > 0 else chips - i // 2)) % chips * 2 + (e + i) % 2

    experts_far_first = sorted(range(1, ne), key=lambda i: (-min(i // 2, chips - i // 2), i))

    def along_z(d):
        return (((z + (1, nz - 1)[d]) % nz) * nx + x, e)

    def along_x(d):
        return (z * nx + (x + (1, nx - 1)[d]) % nx, e)

    def expert(i):
        return (s, owner(i, 1))

    def remote(src, dst, send, recv, to):
        return pltpu.make_async_remote_copy(
            src_ref=src, dst_ref=dst, send_sem=send, recv_sem=recv, device_id=to, device_id_type=MESH
        )

    def arrived(dst, recv):
        remote(dst, dst, recv, recv, along_z(0)).wait_recv()

    def sent(src, send):
        remote(src, src, send, send, along_z(0)).wait_send()

    weights = [
        pltpu.make_async_copy(h.at[0], v, w_sem.at[i]) for i, (h, v) in enumerate(((wg_hbm, wg), (wu_hbm, wu), (wd_hbm, wd)))
    ]
    for copy in weights:
        copy.start()

    barrier = pltpu.get_barrier_semaphore()

    def greet(i, carry):
        pl.semaphore_signal(barrier, inc=1, device_id=(peer(i), e), device_id_type=MESH)
        return carry

    lax.fori_loop(1, ns, greet, 0)
    for i in range(1, ne):
        pl.semaphore_signal(barrier, inc=1, device_id=expert(i), device_id_type=MESH)

    def mixer(taps, toep, zrows, zpad, crows):
        for j, ref in enumerate((q_ref, k_ref, v_ref)):
            edge[2 * j : 2 * j + 2] = ref[tok - 16 :, :].astype(F32)[14:]
            ext[j, 8 : 8 + tok] = ref[...].astype(F32)
        zpad[...] = jnp.zeros_like(zpad)
        position = lax.broadcasted_iota(jnp.int32, (chans, length), 1).astype(F32)
        decay = column(decay_ref[...])
        root = jnp.sqrt(less_one(-2.0 * decay * length) / less_one(-2.0 * decay))
        scaled = raw_ref[...] * jnp.exp(-decay * position) / root
        for c in range(chans):
            taps[c] = jnp.broadcast_to(scaled[c : c + 1, :], (8, length))

        band = lax.broadcasted_iota(jnp.int32, (tok, tok), 1) >= lax.broadcasted_iota(jnp.int32, (tok, tok), 0)

        def bands(c, carry):
            before = jnp.zeros((tok, tok), F32)
            for k in range(ns):
                row = jnp.concatenate([taps[c, :, k * tok : (k + 1) * tok]] * (tok // 8), axis=0)
                turned = pltpu.roll(row, 0, axis=1, stride=1, stride_axis=0)
                full = jnp.where(band, turned, before)
                toep[c, k * tok : (k + 1) * tok, :] = full.astype(BF16)
                before = turned
            return carry

        early = chans // 4
        lax.fori_loop(0, early, bands, 0)
        slot_maps(routes_ref, picks_ref, place, wmap, ne, cap)
        pl.semaphore_wait(barrier, ns - 1 + ne - 1)

        edge[6:8] = jnp.zeros((2, edge.shape[1]), F32)
        rim_copy = remote(edge, rims, rim_send, rim_recv, ((s + 1) % ns, e))
        rim_copy.start()
        lax.fori_loop(early, 2 * early, bands, 0)
        rim_copy.wait()

        def short(j):
            return (
                filt_ref[j, 0:1, :] * ext[j, 8 : 8 + tok]
                + filt_ref[j, 1:2, :] * ext[j, 7 : 7 + tok]
                + filt_ref[j, 2:3, :] * ext[j, 6 : 6 + tok]
            )

        for j in range(3):
            ext[j, 6:8] = jnp.where(s == 0, 0.0, rims[2 * j : 2 * j + 2])
        zed = (short(1) * short(2)).astype(BF16).astype(F32)
        zsend[...] = zed.T.astype(BF16).reshape(ns, chans, tok)
        zrecv[s] = zsend[s]

        for i in far_first:
            remote(zsend.at[peer(i)], zrecv.at[s], z_send, z_recv, (peer(i), e)).start()
        lax.fori_loop(2 * early, chans, bands, 0)
        remote(zrecv.at[1:], zrecv.at[1:], z_recv, z_recv, (peer(1), e)).wait_recv()

        zrows[...] = zrecv[...].astype(F32).reshape(ns * chans, tok)

        def convolve(c):
            zpad[c, ns:] = zrows[pl.ds(c, ns, stride=chans), :]
            total = jnp.zeros((ns, tok), F32)
            for k in range(0, ns, 2):
                two = jnp.concatenate((zpad[c, ns - k : 2 * ns - k], zpad[c, ns - k - 1 : 2 * ns - k - 1]), axis=1).astype(BF16)
                total += jnp.dot(two, toep[c, k * tok : (k + 2) * tok, :], preferred_element_type=F32)
            crows[pl.ds(c, ns, stride=chans), :] = total

        def convolve_some(g, carry):
            for c in range(chans // 4):
                convolve(g * (chans // 4) + c)
            return carry

        lax.fori_loop(0, 4, convolve_some, 0)
        csend[...] = crows[...].astype(BF16).reshape(ns, chans, tok)
        crecv[s] = csend[s]

        for i in far_first:
            remote(csend.at[peer(i)], crecv.at[s], c_send, c_recv, (peer(i), e)).start()
        ext[1, 0:tok] = short(0)
        remote(zsend.at[1:], zsend.at[1:], z_send, z_send, (peer(1), e)).wait_send()
        remote(crecv.at[1:], crecv.at[1:], c_recv, c_recv, (peer(1), e)).wait_recv()
        conv = crecv[...].astype(F32).reshape(ns * chans, tok).T
        mixed[...] = (res_ref[...].astype(F32) + ext[1, 0:tok] * conv).astype(BF16)
        remote(csend.at[1:], csend.at[1:], c_send, c_send, (peer(1), e)).wait_send()

    vmem = pltpu.VMEM
    pl.run_scoped(
        mixer,
        vmem((chans, 8, length), F32),
        vmem((chans, length, tok), BF16),
        vmem((ns * chans, tok), F32),
        vmem((chans, 2 * ns, tok), F32),
        vmem((ns * chans, tok), F32),
    )

    def experts(acc_g, acc_u, hid, pc, pd):
        picked = jnp.dot(place[...], mixed[...], preferred_element_type=F32)
        outg[...] = picked.reshape(ne, cap, chunk).astype(BF16)
        for i in experts_far_first:
            remote(outg.at[owner(i, 1)], arr.at[e], go_send.at[i], go_recv.at[i], expert(i)).start()
        arr[e] = outg[e]
        acc_g[...] = jnp.zeros_like(acc_g)
        acc_u[...] = jnp.zeros_like(acc_u)
        own = outg[e].astype(F32)
        squares = own * own
        for i in reversed(experts_far_first):
            source = owner(i, -1)
            arrived(arr.at[source], go_recv.at[i])
            values = arr[source].astype(F32)
            squares += values * values
        scale = lax.rsqrt(jnp.sum(squares, axis=-1, keepdims=True) / width + 1e-06)
        spans = []
        for d in range(2):
            spans.append((xa, pc, d, d * wa, wa))
            spans.append((xb, pd, d, 2 * wa + d * wb, wb))
        for c in range(ne):
            values = (arr[c].astype(F32) * scale * gain_ref[:, c * chunk : (c + 1) * chunk]).astype(BF16)
            for ref, _, d, start, size in spans:
                lo, hi = max(start, c * chunk), min(start + size, (c + 1) * chunk)
                if lo < hi:
                    ref[d, 0, 0, :, lo - start : hi - start] = values[:, lo - c * chunk : hi - c * chunk]

        def a_along_z(d, t, j):
            remote(xa.at[d, t, j], xa.at[d, t + 1, j], az_send.at[d], a_recv.at[d, t + 1, j], along_z(d)).start()

        def a_along_x(d, j):
            remote(xa.at[d, 0, j], xa.at[d, 0, j + 1], ax_send.at[d], a_recv.at[d, 0, j + 1], along_x(d)).start()

        def b_along_z(d, t):
            remote(xb.at[d, t, 0], xb.at[d, t + 1, 0], bz_send.at[d], b_recv.at[d, t + 1, 0], along_z(d)).start()

        def b_along_x(d, t, j):
            remote(xb.at[d, t, j], xb.at[d, t, j + 1], bx_send.at[d], b_recv.at[d, t, j + 1], along_x(d)).start()

        for d in range(2):
            b_along_z(d, 0)
            a_along_x(d, 0)
        for d in range(2):
            b_along_x(d, 0, 0)
            a_along_z(d, 0, 0)

        def turned(j, d):
            return (nx - j) % nx if d else j

        def rows_of(ref, d, t):
            parts = [ref[d, t, turned(j, d)].astype(F32) for j in range(nx)]
            return jnp.concatenate(parts, axis=0).astype(BF16)

        def group(d, t):
            return (nz - t) % nz if d else t

        def across(rows, w):
            return lax.dot_general(rows, w, (((1,), (1,)), ((), ())), preferred_element_type=F32)

        def project(d, t):
            at = group(d, t)
            left, right = rows_of(xa, d, t), rows_of(xb, d, t)
            one = slice(d * wa, (d + 1) * wa)
            two = slice(2 * wa + d * wb, 2 * wa + (d + 1) * wb)
            for total, w in ((acc_g, wg), (acc_u, wu)):
                total[at] += across(left, w[:, one]) + across(right, w[:, two])

        def activate(d, t):
            at = group(d, t)
            gate = acc_g[at]
            hid[at] = (gate / (1.0 + jnp.exp(-gate)) * acc_u[at]).astype(BF16)

        def gather_step(p, carry):
            for d in range(2):
                @pl.when(p <= nz - 1)
                def _():
                    arrived(xb.at[d, p, 0], b_recv.at[d, p, 0])
                    b_along_x(d, p, 0)

                @pl.when(p < nz - 1)
                def _():
                    b_along_z(d, p)

                @pl.when(p <= nx - 1)
                def _():
                    arrived(xa.at[d, 0, p], a_recv.at[d, 0, p])
                    a_along_z(d, 0, p)

                @pl.when(p < nx - 1)
                def _():
                    a_along_x(d, p)

            for j in range(nx):
                for d in range(2):
                    t = p - j

                    @pl.when((t >= 1) & (t <= nz - 1))
                    def _():
                        arrived(xa.at[d, t, j], a_recv.at[d, t, j])

                    @pl.when((t >= 1) & (t < nz - 1))
                    def _():
                        a_along_z(d, t, j)

                if j >= 1:
                    for d in range(2):
                        t = p - j

                        @pl.when((t >= 0) & (t <= nz - 1))
                        def _():
                            arrived(xb.at[d, t, j], b_recv.at[d, t, j])
                            if j < nx - 1:
                                b_along_x(d, t, j)

            @pl.when(p == nx - 1)
            def _():
                for copy in weights:
                    copy.wait()

            for d in range(2):
                t = p - (nx - 1)

                @pl.when((t >= 0) & (t < nz - 1))
                def _():
                    project(d, t)

                @pl.when((t > nz // 2) & (t < nz - 1) | ((t == 0) | (t == nz // 2)) & (d == 1))
                def _():
                    activate(d, t)

            return carry

        lax.fori_loop(1, nz + nx - 1, gather_step, 0)

        def down(d, q):
            at = group(d, q % nz)
            rows = hid[at]
            for ref, start, size in ((pc, d * wa, wa), (pd, 2 * wa + d * wb, wb)):
                part = jnp.dot(rows, wd[:, start : start + size], preferred_element_type=F32)
                for j in range(nx):
                    ref[d, q - 1, turned(j, d)] = part[j * cap : (j + 1) * cap].astype(BF16)

        def add(total, more):
            total[...] = (total[...].astype(F32) + more[...].astype(F32)).astype(BF16)

        def sum_wide(p, d):
            for v in range(1, nx + 1):
                k, j = p - v + 1, v % nx

                @pl.when((k >= 1) & (k <= nz))
                def _():
                    if v >= 2:
                        arrived(rd1.at[d, v - 2, k - 1], rd1_recv.at[d, v - 2, k - 1])
                        add(pd.at[d, k - 1, j], rd1.at[d, v - 2, k - 1])
                    if v < nx:
                        remote(
                            pd.at[d, k - 1, j], rd1.at[d, v - 1, k - 1], dx_send.at[d], rd1_recv.at[d, v - 1, k - 1], along_x(d)
                        ).start()
                    else:
                        @pl.when(k >= 2)
                        def _():
                            arrived(rd2.at[d, k - 2], rd2_recv.at[d, k - 2])
                            add(pd.at[d, k - 1, 0], rd2.at[d, k - 2])

                        @pl.when(k < nz)
                        def _():
                            remote(
                                pd.at[d, k - 1, 0], rd2.at[d, k - 1], dz_send.at[d], rd2_recv.at[d, k - 1], along_z(d)
                            ).start()

        def sum_narrow(p, d):
            for v in range(1, nx + 1):
                q, j = p - v + 1, v % nx

                @pl.when((q >= 2) & (q <= nz))
                def _():
                    arrived(rc1.at[d, q - 2, j], rc1_recv.at[d, q - 2, j])
                    add(pc.at[d, q - 1, j], rc1.at[d, q - 2, j])

                @pl.when((q >= 1) & (q < nz))
                def _():
                    remote(
                        pc.at[d, q - 1, j], rc1.at[d, q - 1, j], cz_send.at[d], rc1_recv.at[d, q - 1, j], along_z(d)
                    ).start()

                @pl.when(q == nz)
                def _():
                    if v >= 2:
                        arrived(rc2.at[d, v - 2], rc2_recv.at[d, v - 2])
                        add(pc.at[d, nz - 1, j], rc2.at[d, v - 2])
                    if v < nx:
                        remote(
                            pc.at[d, nz - 1, j], rc2.at[d, v - 1], cx_send.at[d], rc2_recv.at[d, v - 1], along_x(d)
                        ).start()

        for d in (1, 0):
            project(d, nz - 1)
            activate(d, nz - 1)
            down(1 - d, 1)
            sum_wide(1, 1 - d)
            sum_narrow(1, 1 - d)
        for d in range(2):
            down(d, 2)

        def reduce_step(p, carry):
            for d in range(2):
                sum_wide(p, d)
            for d in range(2):
                sum_narrow(p, d)
            for d in range(2):
                @pl.when(p < nz)
                def _():
                    down(d, p + 1)

            return carry

        lax.fori_loop(2, nz + nx, reduce_step, 0)

        for c in range(ne):
            for _, ref, d, start, size in spans:
                lo, hi = max(start, c * chunk), min(start + size, (c + 1) * chunk)
                if lo < hi:
                    yb[c, :, lo - c * chunk : hi - c * chunk] = ref[d, nz - 1, 0, :, lo - start : hi - start]
        for i in experts_far_first:
            remote(yb.at[owner(i, 1)], ret.at[e], back_send.at[i], back_recv.at[i], expert(i)).start()
        ret[e] = yb[e]
        for d in range(2):
            sent(xa.at[d, 0 : nz - 1], az_send.at[d])
            sent(xa.at[d, 0, 0 : nx - 1], ax_send.at[d])
            sent(xb.at[d, 0 : nz - 1, 0], bz_send.at[d])
            sent(xb.at[d, :, 0 : nx - 1], bx_send.at[d])
            sent(pc.at[d, 0 : nz - 1], cz_send.at[d])
            sent(pc.at[d, nz - 1, 0 : nx - 1], cx_send.at[d])
            sent(pd.at[d, 0 : nz - 1, 0], dz_send.at[d])
            sent(pd.at[d, :, 0 : nx - 1], dx_send.at[d])
        for i in range(1, ne):
            sent(outg.at[i], go_send.at[i])
        for i in range(1, ne):
            arrived(ret.at[owner(i, -1)], back_recv.at[i])
        rows = ret[...].astype(F32).reshape(ne * cap, chunk)
        combined = lax.dot_general(
            wmap[...], rows, (((0,), (0,)), ((), ())), preferred_element_type=F32, precision=lax.Precision.HIGHEST
        )
        out_ref[...] = mixed[...].astype(F32) + combined
        for i in range(1, ne):
            sent(yb.at[i], back_send.at[i])

    hidden = wd.shape[0]
    pl.run_scoped(
        experts,
        vmem((nz, nx * cap, hidden), F32),
        vmem((nz, nx * cap, hidden), F32),
        vmem((nz, nx * cap, hidden), BF16),
        vmem((2, nz, nx, cap, wa), BF16),
        vmem((2, nz, nx, cap, wb), BF16),
    )


def block(residual, query, key, value, short_kernel, raw, decay, routes, picks, gain, w_gate, w_up, w_down, nz, nx, parts):
    ns, ne = nz * nx, lax.axis_size("exp")
    tok, chunk = query.shape
    chans, length = raw.shape
    cap = 5 * tok * routes.shape[0] // (4 * ne)
    width = ne * chunk
    wa, wb = parts
    hidden = w_gate.shape[1]
    vmem, dma = pltpu.VMEM, pltpu.SemaphoreType.DMA
    scratch = [
        vmem((tok, chunk), BF16),
        vmem((ne * cap, tok), BF16),
        vmem((ne * cap, tok), F32),
        vmem((3, 8 + tok, chunk), F32),
        vmem((8, chunk), F32),
        vmem((8, chunk), F32),
    ]
    scratch += [vmem((ns, chans, tok), BF16)] * 4
    scratch += [vmem((hidden, width), BF16)] * 3
    scratch += [
        vmem((ne, cap, chunk), BF16),
        vmem((ne, cap, chunk), BF16),
        vmem((2, nz, nx, cap, wa), BF16),
        vmem((2, nz, nx, cap, wb), BF16),
        vmem((2, nz - 1, nx, cap, wa), BF16),
        vmem((2, nx - 1, cap, wa), BF16),
        vmem((2, nx - 1, nz, cap, wb), BF16),
        vmem((2, nz - 1, cap, wb), BF16),
        vmem((ne, cap, chunk), BF16),
        vmem((ne, cap, chunk), BF16),
    ]
    scratch += [dma] * 6
    scratch += [
        dma((3,)),
        dma((ne,)),
        dma((ne,)),
        dma((2, nz, nx)),
        dma((2, nz, nx)),
        dma((2, nz - 1, nx)),
        dma((2, nx - 1)),
        dma((2, nx - 1, nz)),
        dma((2, nz - 1)),
        dma((ne,)),
        dma((ne,)),
    ] + [dma((2,))] * 8
    return pl.pallas_call(
        functools.partial(block_kernel, (nz, nx, ne, cap, wa, wb)),
        out_shape=jax.ShapeDtypeStruct((tok, chunk), F32),
        in_specs=[pl.BlockSpec(memory_space=pltpu.VMEM)] * 10 + [pl.BlockSpec(memory_space=pl.ANY)] * 3,
        out_specs=pl.BlockSpec(memory_space=pltpu.VMEM),
        scratch_shapes=scratch,
        compiler_params=pltpu.CompilerParams(
            collective_id=0, has_side_effects=True, vmem_limit_bytes=61 * 1024 * 1024
        ),
    )(residual, query, key, value, short_kernel, raw, decay, routes, picks, gain, w_gate, w_up, w_down)


def on_device(
    residual,
    query_proj,
    key_proj,
    value_proj,
    short_kernel,
    filter_raw,
    filter_decay,
    routes,
    gate_weights,
    norm_gain,
    w_gate,
    w_up,
    w_down,
):
    return block(
        residual,
        query_proj,
        key_proj,
        value_proj,
        short_kernel,
        filter_raw[:, 0, :].T,
        filter_decay,
        routes.T,
        gate_weights.T,
        norm_gain[None, :],
        jnp.swapaxes(w_gate, 1, 2),
        jnp.swapaxes(w_up, 1, 2),
        w_down,
        lax.axis_size("seq") // 4,
        4,
        (768, 1280),
    ).astype(BF16)


def solution(mesh):
    in_specs = (
        P("seq", "exp"),
        P("seq", "exp"),
        P("seq", "exp"),
        P("seq", "exp"),
        P(None, None, "exp"),
        P(None, "exp", "seq"),
        P("exp", "seq"),
        P("seq", None),
        P("seq", None),
        P(),
        P("exp", None, "seq"),
        P("exp", None, "seq"),
        P("exp", "seq", None),
    )
    out_specs = P("seq", "exp")
    return jax.shard_map(
        on_device, mesh=mesh, in_specs=in_specs, out_specs=out_specs, check_vma=False
    )
```

```python
import functools

import jax
import jax.numpy as jnp
from jax import lax
from jax.experimental import pallas as pl
from jax.experimental.pallas import tpu as pltpu
from jax.sharding import PartitionSpec as P

MESH = pl.DeviceIdType.MESH
F32, BF16 = jnp.float32, jnp.bfloat16


def column(row):
    n = row.shape[1]
    same = lax.broadcasted_iota(jnp.int32, (n, n), 0) == lax.broadcasted_iota(jnp.int32, (n, n), 1)
    return jnp.sum(jnp.where(same, jnp.broadcast_to(row, (n, n)), 0.0), axis=1, keepdims=True)


def less_one(v):
    series = jnp.ones_like(v)
    for n in range(11, 1, -1):
        series = 1.0 + v * (1.0 / n) * series
    return jnp.where(v > -0.5, v * series, jnp.exp(v) - 1.0)


def slot_maps(routes_ref, picks_ref, place, wmap, keys, ne, cap):
    topk, tok = routes_ref.shape
    routes = routes_ref[...]
    ids = lax.broadcasted_iota(jnp.int32, (ne, tok), 0)
    hot = [(ids == routes[k : k + 1]).astype(F32) for k in range(topk)]
    before = lax.broadcasted_iota(jnp.int32, (tok, tok), 0) < lax.broadcasted_iota(jnp.int32, (tok, tok), 1)
    earlier = jnp.dot(sum(hot).astype(BF16), before.astype(F32).astype(BF16), preferred_element_type=F32)
    row = lax.broadcasted_iota(jnp.int32, (ne * cap, tok), 0).astype(F32)
    marks, weights = 0.0, 0.0
    keys[...] = jnp.zeros_like(keys)
    for k in range(topk):
        key = routes[k : k + 1].astype(F32) * cap + jnp.sum(hot[k] * earlier, axis=0, keepdims=True)
        keys[k : k + 1] = key
        marks += jnp.where(row == key, 1.0, 0.0)
        weights += jnp.where(row == key, picks_ref[k : k + 1, :], 0.0)
    place[...] = marks.astype(BF16)
    wmap[...] = weights


def block_kernel(
    dims,
    res_ref, q_ref, k_ref, v_ref, filt_ref, raw_ref, decay_ref, routes_ref, picks_ref, gain_ref, wg_hbm, wu_hbm, wd_hbm,
    out_ref,
    mixed, place, wmap, ext, rims, edge, zsend, zrecv, csend, crecv,
    wg, wu, wd, gain, outg, arr, xa, xb, fr, fk, fs, xf, rc1, rc2, rd1, rd2, yb, ret,
    rim_send, rim_recv, z_send, z_recv, c_send, c_recv,
    w_sem, go_send, go_recv, a_recv, b_recv, rc1_recv, rc2_recv, rd1_recv, rd2_recv, back_send, back_recv,
    az_send, ax_send, bz_send, bx_send, cz_send, cx_send, dz_send, dx_send,
    fr_recv, fk_recv, f_recv, f_send, fr_send, fk_send,
):
    nz, nx, ne, cap, wa, wb = dims
    width = 2 * (wa + wb)
    chunk = width // ne
    few = chunk // 4
    rest = chunk - few
    ga = ne * rest * 5 // 24
    gb = ne * rest // 2 - ga
    ns, tok = nz * nx, q_ref.shape[0]
    chans, length = raw_ref.shape
    s, e = lax.axis_index("seq"), lax.axis_index("exp")
    z, x = s // nx, s % nx

    def peer(i):
        return (z + i // nx) % nz * nx + (x + i % nx) % nx

    def hops(i):
        return min(i // nx, nz - i // nx) + min(i % nx, nx - i % nx)

    far_first = sorted(range(1, ns), key=lambda i: -hops(i))
    chips = ne // 2

    def owner(i, way):
        return (e // 2 + (i // 2 if way > 0 else chips - i // 2)) % chips * 2 + (e + i) % 2

    experts_far_first = sorted(range(1, ne), key=lambda i: (-min(i // 2, chips - i // 2), i))

    def along_z(d):
        return (((z + (1, nz - 1)[d]) % nz) * nx + x, e)

    def along_x(d):
        return (z * nx + (x + (1, nx - 1)[d]) % nx, e)

    def expert(i):
        return (s, owner(i, 1))

    def remote(src, dst, send, recv, to):
        return pltpu.make_async_remote_copy(
            src_ref=src, dst_ref=dst, send_sem=send, recv_sem=recv, device_id=to, device_id_type=MESH
        )

    def arrived(dst, recv):
        remote(dst, dst, recv, recv, along_z(0)).wait_recv()

    def sent(src, send):
        remote(src, src, send, send, along_z(0)).wait_send()

    columns = []
    for c in range(ne):
        columns.append((few * c, chunk * c, few))
        columns.append((ne * few + rest * c, chunk * c + few, rest))
    weights = [pltpu.make_async_copy(wd_hbm.at[0], wd, w_sem.at[2])]
    weights[0].start()
    for i, (h, v) in enumerate(((wg_hbm, wg), (wu_hbm, wu))):
        for new, old, size in columns:
            pltpu.make_async_copy(h.at[0, :, old : old + size], v.at[:, new : new + size], w_sem.at[i]).start()
        weights.append(pltpu.make_async_copy(h.at[0], v, w_sem.at[i]))
    for new, old, size in columns:
        gain[:, new : new + size] = gain_ref[:, old : old + size]

    barrier = pltpu.get_barrier_semaphore()

    def greet(i, carry):
        pl.semaphore_signal(barrier, inc=1, device_id=(peer(i), e), device_id_type=MESH)
        return carry

    lax.fori_loop(1, ns, greet, 0)
    for i in range(1, ne):
        pl.semaphore_signal(barrier, inc=1, device_id=expert(i), device_id_type=MESH)

    def mixer(taps, toep, zrows, zpad, crows):
        for j, ref in enumerate((q_ref, k_ref, v_ref)):
            edge[2 * j : 2 * j + 2] = ref[tok - 16 :, :].astype(F32)[14:]
            ext[j, 8 : 8 + tok] = ref[...].astype(F32)
        zpad[...] = jnp.zeros_like(zpad)
        position = lax.broadcasted_iota(jnp.int32, (chans, length), 1).astype(F32)
        decay = column(decay_ref[...])
        root = jnp.sqrt(less_one(-2.0 * decay * length) / less_one(-2.0 * decay))
        scaled = raw_ref[...] * jnp.exp(-decay * position) / root
        for c in range(chans):
            taps[c] = jnp.broadcast_to(scaled[c : c + 1, :], (8, length))

        band = lax.broadcasted_iota(jnp.int32, (tok, tok), 1) >= lax.broadcasted_iota(jnp.int32, (tok, tok), 0)

        def bands(c, carry):
            before = jnp.zeros((tok, tok), F32)
            for k in range(ns):
                row = jnp.concatenate([taps[c, :, k * tok : (k + 1) * tok]] * (tok // 8), axis=0)
                turned = pltpu.roll(row, 0, axis=1, stride=1, stride_axis=0)
                full = jnp.where(band, turned, before)
                toep[c, k * tok : (k + 1) * tok, :] = full.astype(BF16)
                before = turned
            return carry

        early = chans // 4
        lax.fori_loop(0, early, bands, 0)
        slot_maps(routes_ref, picks_ref, place, wmap, fk.at[0, 0], ne, cap)
        pl.semaphore_wait(barrier, ns - 1 + ne - 1)

        edge[6:8] = jnp.zeros((2, edge.shape[1]), F32)
        rim_copy = remote(edge, rims, rim_send, rim_recv, ((s + 1) % ns, e))
        rim_copy.start()
        lax.fori_loop(early, 2 * early, bands, 0)
        rim_copy.wait()

        def short(j):
            return (
                filt_ref[j, 0:1, :] * ext[j, 8 : 8 + tok]
                + filt_ref[j, 1:2, :] * ext[j, 7 : 7 + tok]
                + filt_ref[j, 2:3, :] * ext[j, 6 : 6 + tok]
            )

        for j in range(3):
            ext[j, 6:8] = jnp.where(s == 0, 0.0, rims[2 * j : 2 * j + 2])
        zed = (short(1) * short(2)).astype(BF16).astype(F32)
        zsend[...] = zed.T.astype(BF16).reshape(ns, chans, tok)
        zrecv[s] = zsend[s]

        for i in far_first:
            remote(zsend.at[peer(i)], zrecv.at[s], z_send, z_recv, (peer(i), e)).start()
        lax.fori_loop(2 * early, chans, bands, 0)
        remote(zrecv.at[1:], zrecv.at[1:], z_recv, z_recv, (peer(1), e)).wait_recv()

        zrows[...] = zrecv[...].astype(F32).reshape(ns * chans, tok)

        def convolve(c):
            zpad[c, ns:] = zrows[pl.ds(c, ns, stride=chans), :]
            total = jnp.zeros((ns, tok), F32)
            for k in range(0, ns, 2):
                two = jnp.concatenate((zpad[c, ns - k : 2 * ns - k], zpad[c, ns - k - 1 : 2 * ns - k - 1]), axis=1).astype(BF16)
                total += jnp.dot(two, toep[c, k * tok : (k + 2) * tok, :], preferred_element_type=F32)
            crows[pl.ds(c, ns, stride=chans), :] = total

        def convolve_some(g, carry):
            for c in range(chans // 4):
                convolve(g * (chans // 4) + c)
            return carry

        lax.fori_loop(0, 4, convolve_some, 0)
        csend[...] = crows[...].astype(BF16).reshape(ns, chans, tok)
        crecv[s] = csend[s]

        for i in far_first:
            remote(csend.at[peer(i)], crecv.at[s], c_send, c_recv, (peer(i), e)).start()
        ext[1, 0:tok] = short(0)
        remote(zsend.at[1:], zsend.at[1:], z_send, z_send, (peer(1), e)).wait_send()
        remote(crecv.at[1:], crecv.at[1:], c_recv, c_recv, (peer(1), e)).wait_recv()
        conv = crecv[...].astype(F32).reshape(ns * chans, tok).T
        mixed[...] = (res_ref[...].astype(F32) + ext[1, 0:tok] * conv).astype(BF16)
        remote(csend.at[1:], csend.at[1:], c_send, c_send, (peer(1), e)).wait_send()

    vmem = pltpu.VMEM
    pl.run_scoped(
        mixer,
        vmem((chans, 8, length), F32),
        vmem((chans, length, tok), BF16),
        vmem((ns * chans, tok), F32),
        vmem((chans, 2 * ns, tok), F32),
        vmem((ns * chans, tok), F32),
    )

    def experts(acc_g, acc_u, acc_s, hid, pc, pd):
        core = e % 2

        def raw_along_z(t):
            to = (z + 1 + core * (nz - 2)) % nz * nx + x
            for ref, send, recv in ((fr, fr_send, fr_recv), (fk, fk_send, fk_recv)):
                remote(ref.at[t, 0], ref.at[t + 1, 0], send.at[0], recv.at[t + 1, 0], (to, e)).start()

        def raw_along_x(t, j):
            to = z * nx + (x + 1 + core * (nx - 2)) % nx
            for ref, send, recv in ((fr, fr_send, fr_recv), (fk, fk_send, fk_recv)):
                remote(ref.at[t, j], ref.at[t, j + 1], send.at[1], recv.at[t, j + 1], (to, e)).start()

        def spread(t, j):
            keys = fk[t, j]
            row = lax.broadcasted_iota(jnp.int32, (ne * cap, tok), 0).astype(F32)
            marks = jnp.where((row == keys[0:1]) | (row == keys[1:2]), 1.0, 0.0).astype(BF16)
            picked = jnp.dot(marks, fr[t, j], preferred_element_type=F32)
            picked = picked.reshape(ne, cap, few).astype(BF16)
            tz, jx = (t + core * (nz - 2 * t)) % nz, (j + core * (nx - 2 * j)) % nx
            for c in range(ne):
                fs[t, c, jx] = picked[c]
            if j == nx - 1:
                for i in experts_far_first:
                    remote(fs.at[t, owner(i, 1)], xf.at[tz, e], f_send, f_recv.at[tz], expert(i)).start()
                xf[tz, e] = fs[t, e]

        def raw_step(h):
            for j in range(nx):
                t = h - j

                @pl.when((t >= 0) & (t <= nz - 1))
                def _():
                    arrived(fr.at[t, j], fr_recv.at[t, j])
                    arrived(fk.at[t, j], fk_recv.at[t, j])
                    if j < nx - 1:
                        raw_along_x(t, j)

                if j == 0:
                    @pl.when(t < nz - 1)
                    def _():
                        raw_along_z(t)

        def spread_step(h):
            for j in range(nx):
                t = h - j

                @pl.when((t >= 0) & (t <= nz - 1))
                def _():
                    spread(t, j)

        fr[0, 0] = mixed[:, :few]
        raw_along_z(0)
        raw_along_x(0, 0)
        picked = jnp.dot(place[...], mixed[:, few:], preferred_element_type=F32)
        outg[...] = picked.reshape(ne, cap, rest).astype(BF16)
        for i in experts_far_first:
            remote(outg.at[owner(i, 1)], arr.at[e], go_send.at[i], go_recv.at[i], expert(i)).start()
        arr[e] = outg[e]
        spread(0, 0)
        raw_step(1)
        acc_g[...] = jnp.zeros_like(acc_g)
        acc_u[...] = jnp.zeros_like(acc_u)
        acc_s[...] = jnp.zeros_like(acc_s)
        for h in range(2, nx):
            raw_step(h)
        for i in reversed(experts_far_first):
            arrived(arr.at[owner(i, -1)], go_recv.at[i])
        for c in range(ne):
            for ref, d, start, size in ((xa, 0, 0, ga), (xa, 1, ga, ga), (xb, 0, 2 * ga, gb), (xb, 1, 2 * ga + gb, gb)):
                lo, hi = max(start, c * rest), min(start + size, (c + 1) * rest)
                if lo < hi:
                    ref[d, 0, 0, :, lo - start : hi - start] = arr[c, :, lo - c * rest : hi - c * rest]
        spans = []
        for d in range(2):
            spans.append((pc, d, d * wa, wa))
            spans.append((pd, d, 2 * wa + d * wb, wb))

        def a_along_z(d, t, j):
            remote(xa.at[d, t, j], xa.at[d, t + 1, j], az_send.at[d], a_recv.at[d, t + 1, j], along_z(d)).start()

        def a_along_x(d, j):
            remote(xa.at[d, 0, j], xa.at[d, 0, j + 1], ax_send.at[d], a_recv.at[d, 0, j + 1], along_x(d)).start()

        def b_along_z(d, t):
            remote(xb.at[d, t, 0], xb.at[d, t + 1, 0], bz_send.at[d], b_recv.at[d, t + 1, 0], along_z(d)).start()

        def b_along_x(d, t, j):
            remote(xb.at[d, t, j], xb.at[d, t, j + 1], bx_send.at[d], b_recv.at[d, t, j + 1], along_x(d)).start()

        for d in range(2):
            b_along_z(d, 0)
            a_along_x(d, 0)
        for d in range(2):
            b_along_x(d, 0, 0)
            a_along_z(d, 0, 0)
        for h in range(1, nx):
            spread_step(h)

        def turned(j, d):
            return (nx - j) % nx if d else j

        def rows_of(ref, d, t):
            parts = [ref[d, t, turned(j, d)].astype(F32) for j in range(nx)]
            return jnp.concatenate(parts, axis=0)

        def group(d, t):
            return (nz - t) % nz if d else t

        def across(rows, w):
            return lax.dot_general(rows, w, (((1,), (1,)), ((), ())), preferred_element_type=F32)

        def take(at, rows, start):
            cols = slice(start, start + rows.shape[1])
            acc_s[at] += jnp.sum(rows * rows, axis=-1, keepdims=True)
            rows = (rows * gain[:, cols]).astype(BF16)
            acc_g[at] += across(rows, wg[:, cols])
            acc_u[at] += across(rows, wu[:, cols])

        def project(d, t):
            at = group(d, t)
            take(at, rows_of(xa, d, t), ne * few + d * ga)
            take(at, rows_of(xb, d, t), ne * few + 2 * ga + d * gb)

        def activate(d, t):
            at = group(d, t)
            arrived(xf.at[at, 0 : ne - 1], f_recv.at[at])
            rows = [jnp.concatenate([xf[at, c, j].astype(F32) for c in range(ne)], axis=1) for j in range(nx)]
            take(at, jnp.concatenate(rows, axis=0), 0)
            scale = lax.rsqrt(acc_s[at] / width + 1e-06)
            gate = acc_g[at] * scale
            hid[at] = (gate / (1.0 + jnp.exp(-gate)) * (acc_u[at] * scale)).astype(BF16)

        def gather_step(p, carry):
            for d in range(2):
                @pl.when(p <= nz - 1)
                def _():
                    arrived(xb.at[d, p, 0], b_recv.at[d, p, 0])
                    b_along_x(d, p, 0)

                @pl.when(p < nz - 1)
                def _():
                    b_along_z(d, p)

                @pl.when(p <= nx - 1)
                def _():
                    arrived(xa.at[d, 0, p], a_recv.at[d, 0, p])
                    a_along_z(d, 0, p)

                @pl.when(p < nx - 1)
                def _():
                    a_along_x(d, p)

            for j in range(nx):
                for d in range(2):
                    t = p - j

                    @pl.when((t >= 1) & (t <= nz - 1))
                    def _():
                        arrived(xa.at[d, t, j], a_recv.at[d, t, j])

                    @pl.when((t >= 1) & (t < nz - 1))
                    def _():
                        a_along_z(d, t, j)

                if j >= 1:
                    for d in range(2):
                        t = p - j

                        @pl.when((t >= 0) & (t <= nz - 1))
                        def _():
                            arrived(xb.at[d, t, j], b_recv.at[d, t, j])
                            if j < nx - 1:
                                b_along_x(d, t, j)

            @pl.when(p <= nz - 1)
            def _():
                raw_step(p + nx - 1)
                spread_step(p + nx - 1)

            @pl.when(p == nx - 1)
            def _():
                for copy in weights:
                    copy.wait()

            for d in range(2):
                t = p - (nx - 1)

                @pl.when((t >= 0) & (t < nz - 1))
                def _():
                    project(d, t)

                @pl.when((t > nz // 2) & (t < nz - 1) | ((t == 0) | (t == nz // 2)) & (d == 1))
                def _():
                    activate(d, t)

            return carry

        lax.fori_loop(1, nz + nx - 1, gather_step, 0)

        def down(d, q):
            at = group(d, q % nz)
            rows = hid[at]
            for ref, start, size in ((pc, d * wa, wa), (pd, 2 * wa + d * wb, wb)):
                part = jnp.dot(rows, wd[:, start : start + size], preferred_element_type=F32)
                for j in range(nx):
                    ref[d, q - 1, turned(j, d)] = part[j * cap : (j + 1) * cap].astype(BF16)

        def add(total, more):
            total[...] = (total[...].astype(F32) + more[...].astype(F32)).astype(BF16)

        def sum_wide(p, d):
            for v in range(1, nx + 1):
                k, j = p - v + 1, v % nx

                @pl.when((k >= 1) & (k <= nz))
                def _():
                    if v >= 2:
                        arrived(rd1.at[d, v - 2, k - 1], rd1_recv.at[d, v - 2, k - 1])
                        add(pd.at[d, k - 1, j], rd1.at[d, v - 2, k - 1])
                    if v < nx:
                        remote(
                            pd.at[d, k - 1, j], rd1.at[d, v - 1, k - 1], dx_send.at[d], rd1_recv.at[d, v - 1, k - 1], along_x(d)
                        ).start()
                    else:
                        @pl.when(k >= 2)
                        def _():
                            arrived(rd2.at[d, k - 2], rd2_recv.at[d, k - 2])
                            add(pd.at[d, k - 1, 0], rd2.at[d, k - 2])

                        @pl.when(k < nz)
                        def _():
                            remote(
                                pd.at[d, k - 1, 0], rd2.at[d, k - 1], dz_send.at[d], rd2_recv.at[d, k - 1], along_z(d)
                            ).start()

        def sum_narrow(p, d):
            for v in range(1, nx + 1):
                q, j = p - v + 1, v % nx

                @pl.when((q >= 2) & (q <= nz))
                def _():
                    arrived(rc1.at[d, q - 2, j], rc1_recv.at[d, q - 2, j])
                    add(pc.at[d, q - 1, j], rc1.at[d, q - 2, j])

                @pl.when((q >= 1) & (q < nz))
                def _():
                    remote(
                        pc.at[d, q - 1, j], rc1.at[d, q - 1, j], cz_send.at[d], rc1_recv.at[d, q - 1, j], along_z(d)
                    ).start()

                @pl.when(q == nz)
                def _():
                    if v >= 2:
                        arrived(rc2.at[d, v - 2], rc2_recv.at[d, v - 2])
                        add(pc.at[d, nz - 1, j], rc2.at[d, v - 2])
                    if v < nx:
                        remote(
                            pc.at[d, nz - 1, j], rc2.at[d, v - 1], cx_send.at[d], rc2_recv.at[d, v - 1], along_x(d)
                        ).start()

        for d in (1, 0):
            project(d, nz - 1)
            activate(d, nz - 1)
            down(1 - d, 1)
            sum_wide(1, 1 - d)
            sum_narrow(1, 1 - d)
        for d in range(2):
            down(d, 2)

        def reduce_step(p, carry):
            for d in range(2):
                sum_wide(p, d)
            for d in range(2):
                sum_narrow(p, d)
            for d in range(2):
                @pl.when(p < nz)
                def _():
                    down(d, p + 1)

            return carry

        lax.fori_loop(2, nz + nx, reduce_step, 0)

        for c in range(ne):
            for ref, d, start, size in spans:
                lo, hi = max(start, c * chunk), min(start + size, (c + 1) * chunk)
                if lo < hi:
                    yb[c, :, lo - c * chunk : hi - c * chunk] = ref[d, nz - 1, 0, :, lo - start : hi - start]
        for i in experts_far_first:
            remote(yb.at[owner(i, 1)], ret.at[e], back_send.at[i], back_recv.at[i], expert(i)).start()
        ret[e] = yb[e]
        for d in range(2):
            for ref, send in ((fr, fr_send), (fk, fk_send)):
                if d == 0:
                    sent(ref.at[0 : nz - 1, 0], send.at[0])
                else:
                    sent(ref.at[:, 0 : nx - 1], send.at[1])
            sent(xa.at[d, 0 : nz - 1], az_send.at[d])
            sent(xa.at[d, 0, 0 : nx - 1], ax_send.at[d])
            sent(xb.at[d, 0 : nz - 1, 0], bz_send.at[d])
            sent(xb.at[d, :, 0 : nx - 1], bx_send.at[d])
            sent(pc.at[d, 0 : nz - 1], cz_send.at[d])
            sent(pc.at[d, nz - 1, 0 : nx - 1], cx_send.at[d])
            sent(pd.at[d, 0 : nz - 1, 0], dz_send.at[d])
            sent(pd.at[d, :, 0 : nx - 1], dx_send.at[d])
        sent(fs.at[:, 0 : ne - 1], f_send)
        for i in range(1, ne):
            sent(outg.at[i], go_send.at[i])
        for i in range(1, ne):
            arrived(ret.at[owner(i, -1)], back_recv.at[i])
        rows = ret[...].astype(F32).reshape(ne * cap, chunk)
        combined = lax.dot_general(
            wmap[...], rows, (((0,), (0,)), ((), ())), preferred_element_type=F32, precision=lax.Precision.HIGHEST
        )
        out_ref[...] = mixed[...].astype(F32) + combined
        for i in range(1, ne):
            sent(yb.at[i], back_send.at[i])

    hidden = wd.shape[0]
    pl.run_scoped(
        experts,
        vmem((nz, nx * cap, hidden), F32),
        vmem((nz, nx * cap, hidden), F32),
        vmem((nz, nx * cap, 1), F32),
        vmem((nz, nx * cap, hidden), BF16),
        vmem((2, nz, nx, cap, wa), BF16),
        vmem((2, nz, nx, cap, wb), BF16),
    )


def block(residual, query, key, value, short_kernel, raw, decay, routes, picks, gain, w_gate, w_up, w_down, nz, nx, parts):
    ns, ne = nz * nx, lax.axis_size("exp")
    tok, chunk = query.shape
    chans, length = raw.shape
    cap = 5 * tok * routes.shape[0] // (4 * ne)
    width = ne * chunk
    wa, wb = parts
    hidden = w_gate.shape[1]
    vmem, dma = pltpu.VMEM, pltpu.SemaphoreType.DMA
    scratch = [
        vmem((tok, chunk), BF16),
        vmem((ne * cap, tok), BF16),
        vmem((ne * cap, tok), F32),
        vmem((3, 8 + tok, chunk), F32),
        vmem((8, chunk), F32),
        vmem((8, chunk), F32),
    ]
    scratch += [vmem((ns, chans, tok), BF16)] * 4
    scratch += [vmem((hidden, width), BF16)] * 3
    few = chunk // 4
    rest = chunk - few
    ga = ne * rest * 5 // 24
    gb = ne * rest // 2 - ga
    scratch += [
        vmem((1, width), F32),
        vmem((ne, cap, rest), BF16),
        vmem((ne, cap, rest), BF16),
        vmem((2, nz, nx, cap, ga), BF16),
        vmem((2, nz, nx, cap, gb), BF16),
        vmem((nz, nx, tok, few), BF16),
        vmem((nz, nx, 8, tok), F32),
        vmem((nz, ne, nx, cap, few), BF16),
        vmem((nz, ne, nx, cap, few), BF16),
        vmem((2, nz - 1, nx, cap, wa), BF16),
        vmem((2, nx - 1, cap, wa), BF16),
        vmem((2, nx - 1, nz, cap, wb), BF16),
        vmem((2, nz - 1, cap, wb), BF16),
        vmem((ne, cap, chunk), BF16),
        vmem((ne, cap, chunk), BF16),
    ]
    scratch += [dma] * 6
    scratch += [
        dma((3,)),
        dma((ne,)),
        dma((ne,)),
        dma((2, nz, nx)),
        dma((2, nz, nx)),
        dma((2, nz - 1, nx)),
        dma((2, nx - 1)),
        dma((2, nx - 1, nz)),
        dma((2, nz - 1)),
        dma((ne,)),
        dma((ne,)),
    ] + [dma((2,))] * 8
    scratch += [dma((nz, nx)), dma((nz, nx)), dma((nz,)), dma, dma((2,)), dma((2,))]
    return pl.pallas_call(
        functools.partial(block_kernel, (nz, nx, ne, cap, wa, wb)),
        out_shape=jax.ShapeDtypeStruct((tok, chunk), F32),
        in_specs=[pl.BlockSpec(memory_space=pltpu.VMEM)] * 10 + [pl.BlockSpec(memory_space=pl.ANY)] * 3,
        out_specs=pl.BlockSpec(memory_space=pltpu.VMEM),
        scratch_shapes=scratch,
        compiler_params=pltpu.CompilerParams(
            collective_id=0, has_side_effects=True, vmem_limit_bytes=61 * 1024 * 1024
        ),
    )(residual, query, key, value, short_kernel, raw, decay, routes, picks, gain, w_gate, w_up, w_down)


def on_device(
    residual,
    query_proj,
    key_proj,
    value_proj,
    short_kernel,
    filter_raw,
    filter_decay,
    routes,
    gate_weights,
    norm_gain,
    w_gate,
    w_up,
    w_down,
):
    return block(
        residual,
        query_proj,
        key_proj,
        value_proj,
        short_kernel,
        filter_raw[:, 0, :].T,
        filter_decay,
        routes.T,
        gate_weights.T,
        norm_gain[None, :],
        jnp.swapaxes(w_gate, 1, 2),
        jnp.swapaxes(w_up, 1, 2),
        w_down,
        lax.axis_size("seq") // 4,
        4,
        (768, 1280),
    ).astype(BF16)


def solution(mesh):
    in_specs = (
        P("seq", "exp"),
        P("seq", "exp"),
        P("seq", "exp"),
        P("seq", "exp"),
        P(None, None, "exp"),
        P(None, "exp", "seq"),
        P("exp", "seq"),
        P("seq", None),
        P("seq", None),
        P(),
        P("exp", None, "seq"),
        P("exp", None, "seq"),
        P("exp", "seq", None),
    )
    out_specs = P("seq", "exp")
    return jax.shard_map(
        on_device, mesh=mesh, in_specs=in_specs, out_specs=out_specs, check_vma=False
    )
```
